32 devices in a mesh: ctx: 8 (over z, x), head: 4 (over y, core).
Axes of the slice: x: 2, y: 2, z: 4, core: 2. Of those that a mesh axis runs over, the one named last changes fastest.
Arguments:
- input_x_channels: bfloat16 [8192, 8192], P('ctx', 'head'), may hold values from -4 to 4
- input_b_channels: bfloat16 [8192, 1024], P('ctx', 'head'), may hold values from -3 to 3
- input_c_channels: bfloat16 [8192, 1024], P('ctx', 'head'), may hold values from -3 to 3
- input_gate_channels: bfloat16 [8192, 8192], P('ctx', 'head'), may hold values from -75 to 75
- raw_step_sizes: float32 [128, 8192], P('head', 'ctx'), may hold values from -7 to 800
- log_decay_rate: float32 [128], P('head'), may hold values from -8 to -2.3
- head_skip_coeff: float32 [128], P('head'), may hold values from 0.5 to 2
- x_conv_taps: bfloat16 [4, 8192], P(None, 'head'), may hold values from -3 to 3
- b_conv_taps: bfloat16 [4, 1024], P(None, 'head'), may hold values from -3 to 3
- c_conv_taps: bfloat16 [4, 1024], P(None, 'head'), may hold values from -3 to 3
- gated_norm_gain: bfloat16 [8192], P('head'), may hold values from 0.099609375 to 1.8984375
- output_weight: bfloat16 [8192, 4096], P('head'), may hold values from -0.0625 to 0.0625
- adapter_down_panels: bfloat16 [48, 8192, 64], P('ctx', 'head'), may hold values from -0.0625 to 0.0625
- adapter_up_panels: bfloat16 [48, 64, 4096], P('ctx', None, 'head'), may hold values from -0.75 to 0.75
- turn_first_token: int32 [16], replicated, may hold values from 0 to 8064, as said below
- tenant_of_turn: int32 [16], replicated, may hold values from 0 to 47
- tenant_panel_index: int32 [48], replicated, may hold values from 0 to 47, each once
Outputs:
- out: bfloat16 [8192, 4096], P('ctx', 'head')
The draws below stay inside these ranges and needn't reach their ends.
Inputs may be any that keep to these rules, and one draw needn't show every extreme that they name: `turn_first_token`: strictly increasing multiples of 128; the first is 0; every aligned block of 1024 tokens holds exactly 2 starts, and in every block but the first the earlier of them lies past the block's first token.
All inputs are finite; a program needn't handle non-finite values.
Results may differ from the reference program's by a relative error of at most 0.014.
Values may be sent and summed in bfloat16 or wider, within the bound.
No kernel may reach another device: no remote copies, remote signals or barrier semaphores. Data moves between devices by JAX's collectives and lax.ppermute only.
A program may use at most 192 MiB of HBM per device.

```python
import math
import jax
import jax.numpy as jnp
import numpy as np
from jax import lax

MODEL_WIDTH = 4096
H = 128
P_SIZE = 64
N = 128
G = 8
K = 4
Q = 128
ADAPTER_RANK = 64
UNIT = 128
TOK_DEV = 1024
TOKENS = 8192
INNER_CHANNELS = 8192
GN = 1024
TENANT_COUNT = 48
TURNS = 16


def head_plan(key):
    picks = jax.random.randint(jax.random.fold_in(key, 101), (H,), 0, 8)
    quick_heads = picks < 4
    uniform_draw = jax.random.uniform(jax.random.fold_in(key, 102), (H,), jnp.float32)
    quick_rate = jnp.exp(math.log(0.03) + uniform_draw * math.log(0.1 / 0.03))
    patient_rate = (0.4 + 0.4 * uniform_draw) / (3.0 * math.sqrt(TOKENS))
    decay_rate = jnp.where(quick_heads, quick_rate, patient_rate)
    spot_places = jax.random.randint(jax.random.fold_in(key, 104), (3,), 0, TOKENS)
    strength = 0.22 + 0.23 * jax.random.uniform(jax.random.fold_in(key, 105), (3, H), jnp.float32)
    surge_steps = strength / decay_rate[None, :]
    return (quick_heads, decay_rate, spot_places, surge_steps)


def draw_log_decay_rate(key, part):
    quick_heads, decay_rate, spot_places, surge_steps = head_plan(key)
    return jnp.log(decay_rate)


def draw_raw_step_sizes(key, part):
    quick_heads, decay_rate, spot_places, surge_steps = head_plan(key)
    uniform_draw = jax.random.uniform(jax.random.fold_in(key, 103), (H, TOKENS), jnp.float32)
    slow_scale = 3.0 / math.sqrt(TOKENS)
    quick_steps = 0.4 + 0.9 * uniform_draw
    slow_steps = slow_scale * (0.5 + uniform_draw)
    step_sizes = jnp.where(quick_heads[:, None], quick_steps, slow_steps)
    places = jnp.arange(TOKENS)
    for which in range(3):
        at_spot = places == spot_places[which]
        step_sizes = jnp.where(at_spot[None, :], surge_steps[which][:, None], step_sizes)
    return step_sizes + jnp.log(-jnp.expm1(-step_sizes))


def draw_input_x_channels(key, part):
    quick_heads, decay_rate, spot_places, surge_steps = head_plan(key)
    noise_key = jax.random.fold_in(key, 106)
    noise_draw = jax.random.truncated_normal(noise_key, -4.0, 4.0, (TOKENS, H, P_SIZE), jnp.float32)
    places = jnp.arange(TOKENS)
    factor = jnp.ones((TOKENS, H), jnp.float32)
    for which in range(3):
        near_spot = (places >= spot_places[which] - (K - 1)) & (places <= spot_places[which])
        factor = factor * jnp.where(near_spot[:, None], 1.0 / surge_steps[which][None, :], 1.0)
    return (noise_draw * factor[:, :, None]).reshape(TOKENS, H * P_SIZE).astype(jnp.bfloat16)


def draw_input_gate_channels(key, part):
    noise_key = jax.random.fold_in(key, 301)
    row_key = jax.random.fold_in(key, 302)
    column_key = jax.random.fold_in(key, 303)
    noise_draw = jax.random.truncated_normal(noise_key, -3.0, 3.0, (TOKENS, H * P_SIZE), jnp.float32)
    row_scale = jnp.exp(jax.random.uniform(row_key, (TOKENS, 1), jnp.float32, math.log(0.5), math.log(5.0)))
    column_scale = jnp.exp(jax.random.uniform(column_key, (1, H * P_SIZE), jnp.float32, math.log(0.5), math.log(5.0)))
    return (noise_draw * row_scale * column_scale).astype(jnp.bfloat16)


def draw_turn_first_token(key, part):
    per_block = TOK_DEV // UNIT
    block_count = TOKENS // TOK_DEV
    first_start = jax.random.randint(jax.random.fold_in(key, 201), (block_count,), 1, per_block - 1)
    first_start = jnp.where(jnp.arange(block_count) == 0, 0, first_start)
    room_left = per_block - 1 - first_start
    extra = jax.random.randint(jax.random.fold_in(key, 202), (block_count,), 0, 1 << 20) % room_left
    second_start = first_start + 1 + extra
    second_start = jnp.where(jnp.arange(block_count) == block_count - 1, per_block - 1, second_start)
    block_base = jnp.arange(block_count) * per_block
    joined = jnp.stack([block_base + first_start, block_base + second_start], axis=1)
    return (UNIT * joined).reshape(-1).astype(jnp.int32)


def set_ends(entries, own_key, least, high):
    place = [jax.random.randint(jax.random.fold_in(own_key, axis), (), 0, length) for axis, length in enumerate(entries.shape)]
    main_axis = entries.shape.index(max(entries.shape))
    neighbour = place[:main_axis] + [(place[main_axis] + 1) % entries.shape[main_axis]] + place[main_axis + 1:]
    return entries.at[tuple(place)].set(least).at[tuple(neighbour)].set(high)


def steps_of(rng, shape, shards, low, high):
    gain = 1.0
    for position, shards_of in shards:
        heights = jax.random.uniform(jax.random.fold_in(jax.random.fold_in(rng, 6), position), (shards_of,), jnp.float32, low / len(shards), high / len(shards))
        gain = gain * jnp.repeat(jnp.exp(heights), shape[position] // shards_of).reshape((-1,) + (1,) * (len(shape) - 1 - position))
    return gain


def rank_bounds(amount, slope):
    loads = [(1 << 20) // math.isqrt(grade ** slope) + 1 for grade in range(1, amount + 1)]
    deviation = 1 + sum(loads) // (1 << 30)
    return np.cumsum(np.array([max(1, weight // deviation) for weight in loads]))


def skewed_ids(stream_key, extent, count, slope):
    table = rank_bounds(count, slope)
    pick = jax.random.randint(jax.random.fold_in(stream_key, 1), extent, 0, int(table[count - 1]))
    grade = jnp.searchsorted(jnp.asarray(table, jnp.int32), pick, side="right")
    return jax.random.permutation(jax.random.fold_in(stream_key, 2), count)[grade].astype(jnp.int32)


def centred(rng, extent, deviation, most, cuts=(), held_as=jnp.bfloat16):
    gain = steps_of(rng, extent, cuts, -0.22, 0.18) if cuts else 1.0
    array = jax.random.normal(rng, extent, jnp.float32) * deviation * gain
    return jnp.minimum(jnp.maximum(array, -most), most).astype(held_as)


def setup_inputs(seed: int = 0) -> dict:
    keys = jax.random.split(jax.random.key(seed), 18)
    return {
        "input_x_channels": draw_input_x_channels(jax.random.fold_in(keys[17], 71), 0),
        "input_b_channels": centred(keys[1], (TOKENS, GN), 0.5, 3.0, ((0, 8), (1, 4))),
        "input_c_channels": centred(keys[2], (TOKENS, GN), 0.5, 3.0, ((0, 8), (1, 4))),
        "input_gate_channels": draw_input_gate_channels(jax.random.fold_in(keys[17], 71), 0),
        "raw_step_sizes": draw_raw_step_sizes(jax.random.fold_in(keys[17], 71), 0),
        "log_decay_rate": draw_log_decay_rate(jax.random.fold_in(keys[17], 71), 0),
        "head_skip_coeff": jnp.clip(0.5 + 1.5 * jax.random.uniform(keys[6], (H,), jnp.float32) ** steps_of(keys[6], (H,), ((0, 4),), -0.2, 0.2), 0.5, 2.0),
        "x_conv_taps": centred(keys[7], (K, INNER_CHANNELS), K ** -0.5, 3.0, ((1, 4),)),
        "b_conv_taps": centred(keys[8], (K, GN), K ** -0.5, 3.0, ((1, 4),)),
        "c_conv_taps": centred(keys[9], (K, GN), K ** -0.5, 3.0, ((1, 4),)),
        "gated_norm_gain": jnp.clip(1.0 + 0.18 * jax.random.normal(keys[10], (INNER_CHANNELS,), jnp.float32), 0.099609375, 1.8984375).astype(jnp.bfloat16),
        "output_weight": centred(keys[11], (INNER_CHANNELS, MODEL_WIDTH), INNER_CHANNELS ** -0.5, 0.0625, ((0, 4),)),
        "adapter_down_panels": centred(keys[12], (TENANT_COUNT, INNER_CHANNELS, ADAPTER_RANK), INNER_CHANNELS ** -0.5, 0.0625, ((0, 8), (1, 4))),
        "adapter_up_panels": centred(keys[13], (TENANT_COUNT, ADAPTER_RANK, MODEL_WIDTH), ADAPTER_RANK ** -0.5, 0.75, ((0, 8), (2, 4))),
        "turn_first_token": draw_turn_first_token(jax.random.fold_in(keys[17], 71), 0),
        "tenant_of_turn": set_ends(skewed_ids(keys[15], (TURNS,), TENANT_COUNT, 2), jax.random.fold_in(keys[15], 3), 0, TENANT_COUNT - 1).astype(jnp.int32),
        "tenant_panel_index": jax.random.permutation(keys[16], TENANT_COUNT).astype(jnp.int32),
    }


highest = lax.Precision.HIGHEST
epsilon = 1e-05

def conv_silu(sequence, weight):
    token_rows = sequence.shape[0]
    conv_edge = weight.shape[0] - 1
    joined = jnp.concatenate([jnp.zeros((conv_edge, sequence.shape[1]), jnp.float32), sequence.astype(jnp.float32)], axis=0)
    total = jnp.zeros((token_rows, sequence.shape[1]), jnp.float32)
    for tap in range(weight.shape[0]):
        total = total + weight[tap].astype(jnp.float32) * joined[tap:tap + token_rows]
    return jax.nn.silu(total).astype(jnp.bfloat16)

def group_layer(inputs):
    x_group, b_group, c_group, z_group, step_group, rate_group, skip_group, gain_group = inputs
    per_group = step_group.shape[0]
    token_rows = x_group.shape[0]
    block_count = token_rows // Q
    x_float = x_group.astype(jnp.float32).reshape(token_rows, per_group, P_SIZE)
    x_blocks = x_float.reshape(block_count, Q, per_group, P_SIZE)
    b_blocks = b_group.astype(jnp.float32).reshape(block_count, Q, N)
    c_blocks = c_group.astype(jnp.float32).reshape(block_count, Q, N)
    step_blocks = step_group.reshape(per_group, block_count, Q).transpose(1, 0, 2)
    running = jnp.cumsum(-step_blocks * rate_group[None, :, None], axis=2)
    causal = jnp.arange(Q)[:, None] >= jnp.arange(Q)[None, :]

    def advance(carried, block_span):
        x_part, b_part, c_part, step_part, run_part = block_span
        scores = jnp.dot(c_part, b_part.T, precision=highest)
        log_gap = run_part[:, :, None] - run_part[:, None, :]
        decay_mat = jnp.where(causal, jnp.exp(jnp.where(causal, log_gap, 0.0)), 0.0)
        mixing = scores[None] * decay_mat * step_part[:, None, :]
        output = jnp.einsum('hqk,khp->qhp', mixing, x_part, precision=highest)
        output = output + jnp.exp(run_part).T[:, :, None] * jnp.einsum('qn,hpn->qhp', c_part, carried, precision=highest)
        tail_weight = jnp.exp(run_part[:, -1:] - run_part) * step_part
        fresh = jnp.einsum('hk,khp,kn->hpn', tail_weight, x_part, b_part, precision=highest)
        return (jnp.exp(run_part[:, -1])[:, None, None] * carried + fresh, output)
    start = jnp.zeros((per_group, P_SIZE, N), jnp.float32)
    _, outputs = lax.scan(advance, start, (x_blocks, b_blocks, c_blocks, step_blocks, running))
    y_value = outputs.reshape(token_rows, per_group, P_SIZE) + skip_group[None, :, None] * x_float
    gated = y_value.reshape(token_rows, per_group * P_SIZE) * jax.nn.silu(z_group.astype(jnp.float32))
    norm_scale = lax.rsqrt(lax.optimization_barrier(jnp.mean(gated * gated, axis=1, keepdims=True)) + epsilon)
    return (gated * norm_scale * gain_group.astype(jnp.float32)).astype(jnp.bfloat16)

def reference(input_x_channels, input_b_channels, input_c_channels, input_gate_channels, raw_step_sizes, log_decay_rate, head_skip_coeff, x_conv_taps, b_conv_taps, c_conv_taps, gated_norm_gain, output_weight, adapter_down_panels, adapter_up_panels, turn_first_token, tenant_of_turn, tenant_panel_index):
    per_group = H // G
    group_width = per_group * P_SIZE
    x_conv = conv_silu(input_x_channels, x_conv_taps)
    b_conv = conv_silu(input_b_channels, b_conv_taps)
    c_conv = conv_silu(input_c_channels, c_conv_taps)
    step_sizes = jax.nn.softplus(raw_step_sizes)
    decay_rate = jnp.exp(log_decay_rate)
    grouped = (x_conv.reshape(TOKENS, G, group_width).transpose(1, 0, 2), b_conv.reshape(TOKENS, G, N).transpose(1, 0, 2), c_conv.reshape(TOKENS, G, N).transpose(1, 0, 2), input_gate_channels.reshape(TOKENS, G, group_width).transpose(1, 0, 2), step_sizes.reshape(G, per_group, TOKENS), decay_rate.reshape(G, per_group), head_skip_coeff.reshape(G, per_group), gated_norm_gain.reshape(G, group_width))
    normed = lax.map(group_layer, grouped)
    y_normed = normed.transpose(1, 0, 2).reshape(TOKENS, H * P_SIZE)
    base_out = jnp.dot(y_normed, output_weight, preferred_element_type=jnp.float32)

    def adapt(unit_index):
        first_token = unit_index * UNIT
        block_span = lax.dynamic_slice_in_dim(y_normed, first_token, UNIT, 0)
        turn_index = jnp.sum((turn_first_token <= first_token).astype(jnp.int32)) - 1
        panel_home_index = tenant_panel_index[tenant_of_turn[turn_index]]
        rank_reduced = jnp.dot(block_span, adapter_down_panels[panel_home_index], preferred_element_type=jnp.float32).astype(jnp.bfloat16)
        return jnp.dot(rank_reduced, adapter_up_panels[panel_home_index], preferred_element_type=jnp.float32)
    adapter_out = lax.map(adapt, jnp.arange(TOKENS // UNIT, dtype=jnp.int32)).reshape(TOKENS, MODEL_WIDTH)
    return (base_out + adapter_out).astype(jnp.bfloat16)
```

```python
import functools

import jax
import jax.numpy as jnp
from jax import lax
from jax.experimental import pallas as pl
from jax.experimental.pallas import tpu as pltpu
from jax.sharding import PartitionSpec as P

P_SIZE = 64
N = 128
K = 4
Q = 128
TURN_DEV = 2
HALO = 16
LANES = 128
PIECES = 4
Y_PARTS = 4

F32 = jnp.float32
BF16 = jnp.bfloat16
epsilon = 1e-05
VMEM_LIMIT = 48 * 1024 * 1024


def params():
    return pltpu.CompilerParams(vmem_limit_bytes=VMEM_LIMIT)


def cost(flops, moved):
    return pl.CostEstimate(flops=int(flops), bytes_accessed=int(moved), transcendentals=0)


def silu(v):
    half = 0.5 * v
    return half + half * jnp.tanh(half)


def conv_rows(current, previous, taps):
    rows = current.shape[0]
    joined = jnp.concatenate([previous, current], axis=0)
    total = taps[K - 1 : K] * current
    for back in range(1, K):
        total = total + taps[K - 1 - back : K - back] * pltpu.roll(joined, back, 0)[8 : 8 + rows]
    return silu(total).astype(BF16)


def two_terms(v):
    high = v.astype(BF16).astype(F32)
    return high, v - high


def pad_rows(stack):
    rows = stack.shape[0]
    if rows % LANES:
        fill = jnp.zeros((LANES - rows % LANES, stack.shape[1]), F32)
        stack = jnp.concatenate([stack, fill], axis=0)
    return stack


def panel_kernel(local_ref, owned_ref, down_ref, up_ref, out_ref):
    turn = pl.program_id(0)
    half = down_ref.shape[1] // 2
    rank = down_ref.shape[2]

    @pl.when(owned_ref[turn] == 1)
    def _():
        out_ref[0, :half, :] = jnp.concatenate(
            [down_ref[0, :half, :], down_ref[0, half:, :]], axis=1
        )
        for part in range(up_ref.shape[2] // LANES):
            out_ref[0, half + part * rank : half + (part + 1) * rank, :] = up_ref[
                0, :, part * LANES : (part + 1) * LANES
            ]

    @pl.when(owned_ref[turn] == 0)
    def _():
        out_ref[...] = jnp.zeros_like(out_ref)


def pack_panels(down, up, local_index, owned):
    turns = local_index.shape[0]
    _, channels, rank = down.shape
    features = up.shape[2]
    rows = channels // 2 + rank * (features // LANES)
    return pl.pallas_call(
        panel_kernel,
        grid_spec=pltpu.PrefetchScalarGridSpec(
            num_scalar_prefetch=2,
            grid=(turns,),
            in_specs=[
                pl.BlockSpec((1, channels, rank), lambda j, loc, own: (loc[j], 0, 0)),
                pl.BlockSpec((1, rank, features), lambda j, loc, own: (loc[j], 0, 0)),
            ],
            out_specs=pl.BlockSpec((1, rows, LANES), lambda j, loc, own: (j, 0, 0)),
        ),
        out_shape=jax.ShapeDtypeStruct((turns, rows, LANES), BF16),
        compiler_params=params(),
        cost_estimate=cost(0, turns * rows * LANES * 4),
        name="pack_panels",
    )(local_index, owned, down, up)


def state_kernel(
    parity_ref, x_ref, b_ref, halo_ref, raw_ref, rate_ref, xt_ref, bt_ref, spread_ref,
    xc_ref, bc_ref, run_ref, shifted_ref, before_ref, start_ref, keep_ref, send_ref,
    x_prev, b_prev, weight, x_weighted, state, decay_product,
):
    block = pl.program_id(0)
    inner = x_ref.shape[1]
    bc_width = b_ref.shape[1]
    groups = bc_width // N
    width = inner // groups

    @pl.when(block == 0)
    def _():
        x_prev[...] = halo_ref[:, :inner].astype(F32)[8:]
        b_prev[...] = halo_ref[:, inner : inner + bc_width].astype(F32)[8:]
        state[...] = jnp.zeros_like(state)
        decay_product[...] = jnp.ones_like(decay_product)

    raw = raw_ref[...]
    step = jnp.maximum(raw, 0.0) + jnp.log1p(jnp.exp(-jnp.abs(raw)))
    change = -step * jnp.exp(rate_ref[...])
    heads = raw.shape[0]
    first = change.astype(BF16)
    rest = change - first.astype(F32)
    second = rest.astype(BF16)
    third = (rest - second.astype(F32)).astype(BF16)
    upper = (
        lax.broadcasted_iota(jnp.int32, (Q, Q), 0) <= lax.broadcasted_iota(jnp.int32, (Q, Q), 1)
    ).astype(F32).astype(BF16)
    sums = jnp.dot(jnp.concatenate([first, second, third], axis=0), upper, preferred_element_type=F32)
    run = sums[:heads] + sums[heads : 2 * heads] + sums[2 * heads :]
    run_ref[...] = run
    shifted_ref[...] = jnp.log(step) - run
    last = run[:, Q - 1 : Q]
    tail = jnp.exp(last - run) * step
    whole = jnp.broadcast_to(jnp.exp(last), (heads, Q))
    columns = pad_rows(jnp.concatenate([*two_terms(tail), *two_terms(whole)], axis=0)).T
    spread = spread_ref[...]
    weight[...] = jnp.dot(columns[:, : 2 * heads].astype(BF16), spread, preferred_element_type=F32)
    decay_row = jnp.dot(
        columns[:16, 2 * heads : 4 * heads].astype(BF16), spread, preferred_element_type=F32
    )[:8]

    bc = conv_rows(b_ref[...].astype(F32), b_prev[...], bt_ref[...].astype(F32))
    b_prev[...] = b_ref[Q - HALO :, :].astype(F32)[8:]
    bc_ref[...] = bc

    def conv_lanes(part, carried):
        lanes = pl.ds(pl.multiple_of(part * LANES, LANES), LANES)
        current = x_ref[:, lanes].astype(F32)
        xc = conv_rows(current, x_prev[:, lanes], xt_ref[:, lanes].astype(F32))
        x_prev[:, lanes] = current[Q - 8 :]
        xc_ref[:, lanes] = xc
        x_weighted[:, lanes] = (xc.astype(F32) * weight[:, lanes]).astype(BF16)
        return carried

    lax.fori_loop(0, inner // LANES, conv_lanes, 0, unroll=2)

    start_ref[...] = decay_product[...]
    decay_product[...] = decay_product[...] * decay_row
    for group in range(groups):
        lanes = slice(group * width, (group + 1) * width)
        fresh = lax.dot_general(
            bc[:, group * N : (group + 1) * N],
            x_weighted[:, lanes],
            (((0,), (0,)), ((), ())),
            preferred_element_type=F32,
        )
        held = state[:, lanes]
        before_ref[:, lanes] = held.astype(BF16)
        state[:, lanes] = held * decay_row[:1, lanes] + fresh

    @pl.when(block == pl.num_programs(0) - 1)
    def _():
        half = inner // 2
        row = lax.broadcasted_iota(jnp.int32, (HALO, half), 0)
        for out_ref, place in ((keep_ref, parity_ref[0]), (send_ref, 1 - parity_ref[0])):
            lanes = pl.ds(pl.multiple_of(place * half, LANES), half)
            out_ref[:N] = state[:, lanes].astype(BF16)
            high, low = two_terms(decay_product[:1, lanes])
            out_ref[N:] = jnp.where(row == 0, high, jnp.where(row == 1, low, 0.0)).astype(BF16)


def local_states(parity, x, b, halo, raw, rate, x_taps, b_taps, spread):
    tokens, inner = x.shape
    bc_width = b.shape[1]
    heads = raw.shape[0]
    blocks = tokens // Q
    half = inner // 2
    whole = lambda c, p: (0, 0)
    rows = lambda c, p: (c, 0)
    columns = lambda c, p: (0, c)
    return pl.pallas_call(
        state_kernel,
        grid_spec=pltpu.PrefetchScalarGridSpec(
            num_scalar_prefetch=1,
            grid=(blocks,),
            in_specs=[
                pl.BlockSpec((Q, inner), rows),
                pl.BlockSpec((Q, bc_width), rows),
                pl.BlockSpec(halo.shape, whole),
                pl.BlockSpec((heads, Q), columns),
                pl.BlockSpec((heads, 1), whole),
                pl.BlockSpec((K, inner), whole),
                pl.BlockSpec((K, bc_width), whole),
                pl.BlockSpec(spread.shape, whole),
            ],
            out_specs=[
                pl.BlockSpec((Q, inner), rows),
                pl.BlockSpec((Q, bc_width), rows),
                pl.BlockSpec((heads, Q), columns),
                pl.BlockSpec((heads, Q), columns),
                pl.BlockSpec((N, inner), rows),
                pl.BlockSpec((8, inner), rows),
                pl.BlockSpec((N + HALO, half), whole),
                pl.BlockSpec((N + HALO, half), whole),
            ],
            scratch_shapes=[
                pltpu.VMEM((8, inner), F32),
                pltpu.VMEM((8, bc_width), F32),
                pltpu.VMEM((Q, inner), F32),
                pltpu.VMEM((Q, inner), BF16),
                pltpu.VMEM((N, inner), F32),
                pltpu.VMEM((8, inner), F32),
            ],
        ),
        out_shape=[
            jax.ShapeDtypeStruct((tokens, inner), BF16),
            jax.ShapeDtypeStruct((tokens, bc_width), BF16),
            jax.ShapeDtypeStruct((heads, tokens), F32),
            jax.ShapeDtypeStruct((heads, tokens), F32),
            jax.ShapeDtypeStruct((blocks * N, inner), BF16),
            jax.ShapeDtypeStruct((blocks * 8, inner), F32),
            jax.ShapeDtypeStruct((N + HALO, half), BF16),
            jax.ShapeDtypeStruct((N + HALO, half), BF16),
        ],
        compiler_params=params(),
        cost_estimate=cost(10e9, 20e6),
        name="local_states",
    )(parity, x, b, halo, raw, rate, x_taps, b_taps, spread)


def mix_kernel(
    first, has_alias, *refs
):
    (
        xc_ref, bc_ref, c_ref, c_prev_ref, halo_ref, run_ref, shifted_ref, before_ref, start_ref,
        gate_ref, skip_ref, ct_ref, spread_ref,
    ) = refs[:13]
    refs = refs[13 + (3 if has_alias else 0) :]
    part_ref, scale_ref, cc_ref, rise = refs
    block = pl.program_id(0) + first
    inner = xc_ref.shape[1]
    bc_width = c_ref.shape[1]
    groups = bc_width // N
    width = inner // groups
    heads = run_ref.shape[0]

    c_halo = halo_ref[:, inner + bc_width :].astype(F32)[8:]
    c_before = jnp.where(block == 0, c_halo, c_prev_ref[...].astype(F32)[8:])
    cc = conv_rows(c_ref[...].astype(F32), c_before, ct_ref[...].astype(F32))
    cc_ref[...] = cc
    run = run_ref[...]
    columns = pad_rows(jnp.concatenate([*two_terms(jnp.exp(run)), run], axis=0)).T
    rise[...] = jnp.dot(
        columns[:, : 2 * heads].astype(BF16), spread_ref[...], preferred_element_type=F32
    )
    causal = lax.broadcasted_iota(jnp.int32, (Q, Q), 0) >= lax.broadcasted_iota(jnp.int32, (Q, Q), 1)
    left = lax.broadcasted_iota(jnp.int32, (Q, LANES), 1) < P_SIZE
    for group in range(groups):
        state_lanes = slice(group * N, (group + 1) * N)
        scores = lax.dot_general(
            cc[:, state_lanes],
            bc_ref[:, state_lanes],
            (((1,), (1,)), ((), ())),
            preferred_element_type=F32,
        )
        scores = jnp.where(causal, scores, 0.0)
        for pair in range(width // LANES):
            lanes = slice(group * width + pair * LANES, group * width + (pair + 1) * LANES)
            mixing = []
            for head in (lanes.start // P_SIZE, lanes.start // P_SIZE + 1):
                gap = columns[:, 2 * heads + head : 2 * heads + head + 1] + shifted_ref[head : head + 1, :]
                mixing.append((scores * jnp.exp(jnp.where(causal, gap, 0.0))).astype(BF16))
            x = xc_ref[:, lanes].astype(F32)
            x_pair = jnp.concatenate(
                [jnp.where(left, x, 0.0).astype(BF16), jnp.where(left, 0.0, x).astype(BF16)], axis=0
            )
            y = jnp.dot(jnp.concatenate(mixing, axis=1), x_pair, preferred_element_type=F32)
            carried = jnp.dot(cc[:, state_lanes], before_ref[:, lanes], preferred_element_type=F32)
            rise_part = rise[:, lanes]
            y = y + rise_part * carried + skip_ref[:, lanes] * x
            gate = silu(gate_ref[:, lanes].astype(F32))
            part_ref[:, lanes] = (y * gate).astype(BF16)
            scale_ref[:, lanes] = (gate * rise_part * start_ref[:1, lanes]).astype(BF16)


def mix(first, count, xc, bc, c, halo, run, shifted, before, start, gate, skip, c_taps, spread, held):
    tokens, inner = xc.shape
    bc_width = c.shape[1]
    heads = run.shape[0]
    whole = lambda i: (0, 0)
    rows = lambda i: (first + i, 0)
    columns = lambda i: (0, first + i)
    per_block = Q // HALO
    any_spec = pl.BlockSpec(memory_space=pl.ANY)
    aliased = list(held) if held is not None else []
    return pl.pallas_call(
        functools.partial(mix_kernel, first, bool(aliased)),
        grid=(count,),
        in_specs=[
            pl.BlockSpec((Q, inner), rows),
            pl.BlockSpec((Q, bc_width), rows),
            pl.BlockSpec((Q, bc_width), rows),
            pl.BlockSpec((HALO, bc_width), lambda i: (jnp.maximum((first + i) * per_block - 1, 0), 0)),
            pl.BlockSpec(halo.shape, whole),
            pl.BlockSpec((heads, Q), columns),
            pl.BlockSpec((heads, Q), columns),
            pl.BlockSpec((N, inner), rows),
            pl.BlockSpec((8, inner), rows),
            pl.BlockSpec((Q, inner), rows),
            pl.BlockSpec((1, inner), whole),
            pl.BlockSpec((K, bc_width), whole),
            pl.BlockSpec(spread.shape, whole),
        ]
        + [any_spec] * len(aliased),
        out_specs=[
            pl.BlockSpec((Q, inner), rows),
            pl.BlockSpec((Q, inner), rows),
            pl.BlockSpec((Q, bc_width), rows),
        ],
        out_shape=[
            jax.ShapeDtypeStruct((tokens, inner), BF16),
            jax.ShapeDtypeStruct((tokens, inner), BF16),
            jax.ShapeDtypeStruct((tokens, bc_width), BF16),
        ],
        input_output_aliases={13 + i: i for i in range(len(aliased))},
        scratch_shapes=[pltpu.VMEM((Q, inner), F32)],
        compiler_params=params(),
        cost_estimate=cost(count * 2e9, count * 3e6),
        name="mix",
    )(xc, bc, c, c, halo, run, shifted, before, start, gate, skip, c_taps, spread, *aliased)


def norm_kernel(parity_ref, part_ref, scale_ref, cc_ref, keep_ref, got_ref, gain_ref, out_ref, state):
    inner = part_ref.shape[1]
    groups = cc_ref.shape[1] // N
    width = inner // groups
    half = inner // 2

    @pl.when(pl.program_id(0) == 0)
    def _():
        for ref, place in ((keep_ref, parity_ref[0]), (got_ref, 1 - parity_ref[0])):
            state[:, pl.ds(pl.multiple_of(place * half, LANES), half)] = ref[...]

    for group in range(groups):
        lanes = slice(group * width, (group + 1) * width)
        carried = jnp.dot(
            cc_ref[:, group * N : (group + 1) * N], state[:, lanes], preferred_element_type=F32
        )
        gated = part_ref[:, lanes].astype(F32) + scale_ref[:, lanes].astype(F32) * carried
        mean = jnp.sum(gated * gated, axis=1, keepdims=True) * (1.0 / width)
        out_ref[:, lanes] = (gated * lax.rsqrt(mean + epsilon) * gain_ref[:, lanes]).astype(BF16)


def finish_norm(parity, part, scale, cc, keep, got, gain):
    tokens, inner = part.shape
    tile = 2 * Q
    whole = lambda i, p: (0, 0)
    rows = lambda i, p: (i, 0)
    return pl.pallas_call(
        norm_kernel,
        grid_spec=pltpu.PrefetchScalarGridSpec(
            num_scalar_prefetch=1,
            grid=(tokens // tile,),
            in_specs=[
                pl.BlockSpec((tile, inner), rows),
                pl.BlockSpec((tile, inner), rows),
                pl.BlockSpec((tile, cc.shape[1]), rows),
                pl.BlockSpec(keep.shape, whole),
                pl.BlockSpec(got.shape, whole),
                pl.BlockSpec((1, inner), whole),
            ],
            out_specs=pl.BlockSpec((tile, inner), rows),
            scratch_shapes=[pltpu.VMEM((N, inner), BF16)],
        ),
        out_shape=jax.ShapeDtypeStruct((tokens, inner), BF16),
        compiler_params=params(),
        cost_estimate=cost(2e9, 13e6),
        name="finish_norm",
    )(parity, part, scale, cc, keep, got, gain)


def project_kernel(places_ref, y_ref, w_ref, send_ref, keep_ref):
    rows = 256
    for which, out_ref in enumerate((send_ref, keep_ref)):

        @pl.when(pl.program_id(0) == which)
        def _(out_ref=out_ref):
            def tile(i, carried):
                at = pl.ds(pl.multiple_of(i * rows, rows), rows)
                out_ref[at, :] = jnp.dot(
                    y_ref[at, :], w_ref[...], preferred_element_type=F32
                ).astype(BF16)
                return carried

            lax.fori_loop(0, y_ref.shape[0] // rows, tile, 0)


def project(places, y, weight, width):
    tokens, inner = y.shape
    whole = lambda i, p: (0, 0)
    return pl.pallas_call(
        project_kernel,
        grid_spec=pltpu.PrefetchScalarGridSpec(
            num_scalar_prefetch=1,
            grid=(2,),
            in_specs=[
                pl.BlockSpec((tokens, inner), whole),
                pl.BlockSpec((inner, width), lambda i, p: (0, p[i])),
            ],
            out_specs=[pl.BlockSpec((tokens, width), whole)] * 2,
        ),
        out_shape=[jax.ShapeDtypeStruct((tokens, width), BF16)] * 2,
        compiler_params=params(),
        cost_estimate=cost(4 * tokens * inner * width, 2 * inner * (tokens + 2 * width)),
        name="project",
    )(places, y, weight)


def low_kernel(slot_ref, y_ref, panel_ref, out_ref):
    half = y_ref.shape[1] // 2
    rank = LANES // 2
    panel = panel_ref[0, :half, :]
    low = (
        jnp.dot(y_ref[:, :half], panel, preferred_element_type=F32)[:, :rank]
        + jnp.dot(y_ref[:, half:], panel, preferred_element_type=F32)[:, rank:]
    )
    fold = low.shape[0] // 2
    out_ref[...] = jnp.concatenate([low[:fold], low[fold:]], axis=1)


def low_part(slots, y, panels):
    tokens, inner = y.shape
    return pl.pallas_call(
        low_kernel,
        grid_spec=pltpu.PrefetchScalarGridSpec(
            num_scalar_prefetch=1,
            grid=(tokens // Q,),
            in_specs=[
                pl.BlockSpec((Q, inner), lambda i, s: (i, 0)),
                pl.BlockSpec((1,) + panels.shape[1:], lambda i, s: (s[i], 0, 0)),
            ],
            out_specs=pl.BlockSpec((Q // 2, LANES), lambda i, s: (i, 0)),
        ),
        out_shape=jax.ShapeDtypeStruct((tokens // 2, LANES), F32),
        compiler_params=params(),
        cost_estimate=cost(1e9, 6e6),
        name="low_part",
    )(slots, y, panels)


def final_kernel(count, slot_ref, own_ref, pair_ref, low_ref, panel_ref, *refs):
    parts, out_ref = refs[:-1], refs[-1]
    features = own_ref.shape[1]
    rank = LANES // 2
    base_row = panel_ref.shape[1] - rank * (features // LANES)
    low = low_ref[...].astype(BF16)
    low = jnp.concatenate([low[:, :rank], low[:, rank:]], axis=0)
    part_width = features // count
    for block in range(features // LANES):
        lanes = slice(block * LANES, (block + 1) * LANES)
        total = jnp.dot(
            low,
            panel_ref[0, base_row + block * rank : base_row + (block + 1) * rank, :],
            preferred_element_type=F32,
        )
        total = total + own_ref[:, lanes].astype(F32) + pair_ref[:, lanes].astype(F32)
        place = lanes.start // part_width
        inside = lanes.start - place * part_width
        for ref in parts[place::count]:
            total = total + ref[:, inside : inside + LANES].astype(F32)
        out_ref[:, lanes] = total.astype(BF16)


def final_sum(slots, own, pair, low, panels, parts, count):
    tokens, features = own.shape
    rows = lambda i, s: (i, 0)
    return pl.pallas_call(
        functools.partial(final_kernel, count),
        grid_spec=pltpu.PrefetchScalarGridSpec(
            num_scalar_prefetch=1,
            grid=(tokens // Q,),
            in_specs=[
                pl.BlockSpec((Q, features), rows),
                pl.BlockSpec((Q, features), rows),
                pl.BlockSpec((Q // 2, LANES), rows),
                pl.BlockSpec((1,) + panels.shape[1:], lambda i, s: (s[i], 0, 0)),
            ]
            + [pl.BlockSpec((Q, features // count), rows)] * len(parts),
            out_specs=pl.BlockSpec((Q, features), rows),
        ),
        out_shape=jax.ShapeDtypeStruct((tokens, features), BF16),
        compiler_params=params(),
        cost_estimate=cost(1e8, 10e6),
        name="final_sum",
    )(slots, own, pair, low, panels, *parts)


def shift_up(block, axis, distance):
    devices = range(lax.axis_size(axis))
    route = [(i, i + distance) for i in devices if i + distance in devices]
    return lax.ppermute(block, axis, route)


def swap(block, axis, bits):
    return lax.ppermute(block, axis, [(i, i ^ bits) for i in range(lax.axis_size(axis))])


def unpacked(packed):
    decay = packed[N : N + 1].astype(F32) + packed[N + 1 : N + 2].astype(F32)
    return packed[:N].astype(F32), decay


def packed(state, decay):
    high = decay.astype(BF16)
    low = (decay - high.astype(F32)).astype(BF16)
    fill = jnp.zeros((HALO - 2, state.shape[1]), BF16)
    return jnp.concatenate([state.astype(BF16), high, low, fill], axis=0)


def local(
    input_x_channels,
    input_b_channels,
    input_c_channels,
    input_gate_channels,
    raw_step_sizes,
    log_decay_rate,
    head_skip_coeff,
    x_conv_taps,
    b_conv_taps,
    c_conv_taps,
    gated_norm_gain,
    output_weight,
    adapter_down_panels,
    adapter_up_panels,
    turn_first_token,
    tenant_of_turn,
    tenant_panel_index,
):
    tokens, inner = input_x_channels.shape
    heads = log_decay_rate.shape[0]
    blocks = tokens // Q
    features = adapter_up_panels.shape[2]
    panel_count = adapter_down_panels.shape[0]
    ctx = lax.axis_index("ctx")
    head = lax.axis_index("head")
    parity = (ctx % 2).astype(jnp.int32)
    parity_arg = parity[None]

    edge = jnp.concatenate(
        [array[tokens - HALO :] for array in (input_x_channels, input_b_channels, input_c_channels)],
        axis=1,
    )
    halo = shift_up(edge, "ctx", 1)

    turn_panels = jnp.take(tenant_panel_index, tenant_of_turn)
    owned = (turn_panels // panel_count == ctx).astype(jnp.int32)
    local_index = jnp.where(owned == 1, turn_panels % panel_count, 0)
    packs = pack_panels(adapter_down_panels, adapter_up_panels, local_index, owned)
    own_packs = lax.psum_scatter(packs, "ctx", scatter_dimension=0, tiled=True)
    earlier_pack = shift_up(own_packs[TURN_DEV - 1 :], "ctx", 1)
    own_starts = lax.dynamic_slice_in_dim(turn_first_token, TURN_DEV * ctx, TURN_DEV, 0)
    block_starts = ctx * tokens + Q * jnp.arange(blocks)
    slots = jnp.sum((block_starts[:, None] >= own_starts[None, :]).astype(jnp.int32), axis=1)
    slots = slots.astype(jnp.int32)

    lane_head = jnp.arange(inner) // P_SIZE
    spread = (jnp.arange(2 * heads)[:, None] % heads == lane_head[None, :]).astype(BF16)
    xc, bc, run, shifted, before, start, keep, send = local_states(
        parity_arg,
        input_x_channels,
        input_b_channels,
        halo,
        raw_step_sizes,
        log_decay_rate[:, None],
        x_conv_taps,
        b_conv_taps,
        spread,
    )
    skip = jnp.repeat(head_skip_coeff, P_SIZE)[None]
    count = blocks // PIECES

    def mix_piece(piece, held):
        return mix(
            piece * count, count, xc, bc, input_c_channels, halo, run, shifted, before, start,
            input_gate_channels, skip, c_conv_taps, spread, held,
        )

    got = swap(send, "ctx", 1)
    held = mix_piece(0, None)
    own_state, own_decay = unpacked(keep)
    got_state, got_decay = unpacked(got)
    first = parity == 0
    first_state = jnp.where(first, own_state, got_state)
    first_decay = jnp.where(first, own_decay, got_decay)
    second_state = jnp.where(first, got_state, own_state)
    second_decay = jnp.where(first, got_decay, own_decay)
    window = second_state + second_decay * first_state
    window_decay = second_decay * first_decay
    pairs = lax.axis_size("ctx") // 2
    distance = 1
    incoming = None
    piece = 1
    while distance < pairs:
        arrived = shift_up(packed(window, window_decay), "ctx", 2 * distance)
        if piece < PIECES:
            held = mix_piece(piece, held)
            piece += 1
        state, decay = unpacked(arrived)
        if incoming is None:
            incoming, incoming_decay = state, decay
        else:
            incoming = incoming + incoming_decay * state
            incoming_decay = incoming_decay * decay
        window = window + window_decay * state
        window_decay = window_decay * decay
        distance *= 2
    incoming_second = first_state + first_decay * incoming
    back = swap(jnp.where(first, incoming_second, incoming).astype(BF16), "ctx", 1)
    kept = jnp.where(first, incoming, incoming_second).astype(BF16)
    while piece < PIECES:
        held = mix_piece(piece, held)
        piece += 1
    part, scale, cc = held
    y_normed = finish_norm(
        parity_arg, part, scale, cc, kept, back, gated_norm_gain.astype(F32)[None]
    )

    y_chips = lax.axis_size("head") // 2
    width = features // Y_PARTS
    parts = []
    for chip in range(1, y_chips):
        other = head ^ (2 * chip)
        for part_index in range(Y_PARTS):
            places = jnp.stack([(other ^ 1) * Y_PARTS + part_index, other * Y_PARTS + part_index])
            to_pair, mine = project(places.astype(jnp.int32), y_normed, output_weight, width)
            from_pair = swap(to_pair, "head", 1)
            both = (mine.astype(F32) + from_pair.astype(F32)).astype(BF16)
            parts.append(swap(both, "head", 2 * chip))
    places = jnp.stack([head ^ 1, head]).astype(jnp.int32)
    to_pair, own = project(places, y_normed, output_weight, features)
    pair = swap(to_pair, "head", 1)

    panels = jnp.concatenate([earlier_pack, own_packs], axis=0)
    low = low_part(slots, y_normed, panels)
    low = low + swap(low, "head", 1)
    low_sent = low.astype(BF16)
    for chip in range(1, y_chips):
        low = low + swap(low_sent, "head", 2 * chip).astype(F32)
    return final_sum(slots, own, pair, low, panels, parts, Y_PARTS)


def solution(mesh):
    in_specs = (
        P("ctx", "head"),
        P("ctx", "head"),
        P("ctx", "head"),
        P("ctx", "head"),
        P("head", "ctx"),
        P("head"),
        P("head"),
        P(None, "head"),
        P(None, "head"),
        P(None, "head"),
        P("head"),
        P("head", None),
        P("ctx", "head", None),
        P("ctx", None, "head"),
        P(),
        P(),
        P(),
    )
    out_specs = P("ctx", "head")
    return jax.shard_map(local, mesh=mesh, in_specs=in_specs, out_specs=out_specs, check_vma=False)
```

```python
import functools

import jax
import jax.numpy as jnp
from jax import lax
from jax.experimental import pallas as pl
from jax.experimental.pallas import tpu as pltpu
from jax.sharding import PartitionSpec as P

P_SIZE = 64
N = 128
K = 4
Q = 128
TURN_DEV = 2
HALO = 16
LANES = 128
PIECES = 4
Y_UNITS = 4
Y_FIRST = 2

F32 = jnp.float32
BF16 = jnp.bfloat16
epsilon = 1e-05
MIB = 1024 * 1024


def params(mib=28):
    return pltpu.CompilerParams(vmem_limit_bytes=mib * MIB)


def cost(microseconds):
    return pl.CostEstimate(flops=int(microseconds * 1e5), bytes_accessed=1, transcendentals=0)


def silu(v):
    half = 0.5 * v
    return half + half * jnp.tanh(half)


def conv_rows(current, previous, taps):
    rows = current.shape[0]
    joined = jnp.concatenate([previous, current], axis=0)
    total = taps[K - 1 : K] * current
    for back in range(1, K):
        total = total + taps[K - 1 - back : K - back] * pltpu.roll(joined, back, 0)[8 : 8 + rows]
    return silu(total).astype(BF16)


def two_terms(v):
    high = v.astype(BF16).astype(F32)
    return high, v - high


def column_of(row):
    size = row.shape[1]
    here = lax.broadcasted_iota(jnp.int32, (size, size), 0)
    there = lax.broadcasted_iota(jnp.int32, (size, size), 1)
    return jnp.sum(jnp.where(here == there, row, 0.0), axis=1, keepdims=True)


def pad_rows(stack):
    rows = stack.shape[0]
    if rows % LANES:
        fill = jnp.zeros((LANES - rows % LANES, stack.shape[1]), F32)
        stack = jnp.concatenate([stack, fill], axis=0)
    return stack


def edge_kernel(x_ref, b_ref, c_ref, out_ref):
    place = 0
    for ref in (x_ref, b_ref, c_ref):
        out_ref[:, place : place + ref.shape[1]] = ref[...]
        place += ref.shape[1]


def sequence_edge(*arrays):
    tokens = arrays[0].shape[0]
    width = sum(array.shape[1] for array in arrays)
    return pl.pallas_call(
        edge_kernel,
        grid=(1,),
        in_specs=[
            pl.BlockSpec((HALO, array.shape[1]), lambda i: (tokens // HALO - 1, 0)) for array in arrays
        ],
        out_specs=pl.BlockSpec((HALO, width), lambda i: (0, 0)),
        out_shape=jax.ShapeDtypeStruct((HALO, width), BF16),
        compiler_params=params(62),
        cost_estimate=cost(1),
        name="sequence_edge",
    )(*arrays)


def turn_home(place, bits, slot, count, panel_index, tenants, me):
    relative = 0
    for order, bit in enumerate(bits):
        relative = relative + bit * (1 - (place >> (len(bits) - 1 - order)) % 2)
    panel = panel_index[tenants[TURN_DEV * (relative ^ me) + slot]]
    owned = lax.div(panel, count) == me
    return jnp.where(owned, lax.rem(panel, count), 0), owned


def place_panel(in_ref, out_ref, first, owned):
    rows = slice(first, first + in_ref.shape[1])

    @pl.when(owned)
    def _():
        out_ref[0, rows, :] = in_ref[0]

    @pl.when(jnp.logical_not(owned))
    def _():
        out_ref[0, rows, :] = jnp.zeros_like(in_ref[0])


def panel_kernel(homes, index_ref, tenant_ref, me_ref, *refs):
    place = pl.program_id(0)
    half = pl.num_programs(0) // 2
    ins = list(refs[: sum(len(job) for job in homes)])
    outs = refs[len(ins) :]
    for number, job in enumerate(homes):
        send_ref, keep_ref = outs[2 * number : 2 * number + 2]
        for slot, home in enumerate(job):
            in_ref = ins.pop(0)
            owned = home(place, index_ref, tenant_ref, me_ref[0])[1]
            first = slot * in_ref.shape[1]

            @pl.when(place < half)
            def _(in_ref=in_ref, send_ref=send_ref, owned=owned, first=first):
                place_panel(in_ref, send_ref, first, owned)

            @pl.when(place >= half)
            def _(in_ref=in_ref, keep_ref=keep_ref, owned=owned, first=first):
                place_panel(in_ref, keep_ref, first, owned)


def pack_panels(jobs, panel_index, tenants, me, devices):
    half = devices // 2
    homes, ins, in_specs, out_specs, out_shape = [], [], [], [], []
    for panels, bits, slots in jobs:
        count, rows, width = panels.shape
        homes.append([])
        for slot in slots:

            def home(place, index, tenant, own, bits=bits, slot=slot, count=count):
                return turn_home(place, bits, slot, count, index, tenant, own)

            def at(q, index, tenant, own, home=home):
                return (home(q, index, tenant, own[0])[0], 0, 0)

            homes[-1].append(home)
            ins.append(panels)
            in_specs.append(pl.BlockSpec((1, rows, width), at))
        block = (1, len(slots) * rows, width)
        out_specs.append(pl.BlockSpec(block, lambda q, index, tenant, own: (jnp.minimum(q, half - 1), 0, 0)))
        out_specs.append(pl.BlockSpec(block, lambda q, index, tenant, own: (jnp.maximum(q - half, 0), 0, 0)))
        out_shape += [jax.ShapeDtypeStruct((half,) + block[1:], BF16)] * 2
    outs = pl.pallas_call(
        functools.partial(panel_kernel, homes),
        grid_spec=pltpu.PrefetchScalarGridSpec(
            num_scalar_prefetch=3, grid=(devices,), in_specs=in_specs, out_specs=out_specs
        ),
        out_shape=out_shape,
        compiler_params=params(62),
        cost_estimate=cost(5),
        name="pack_panels",
    )(panel_index, tenants, me, *ins)
    return [outs[2 * job : 2 * job + 2] for job in range(len(jobs))]


def state_kernel(
    parity_ref, x_ref, b_ref, even_ref, odd_ref, raw_ref, rate_ref, xt_ref, bt_ref, spread_ref,
    xc_ref, bc_ref, run_ref, shifted_ref, before_ref, start_ref, keep_ref, send_ref,
    x_prev, b_prev, weight, x_weighted, state, decay_product,
):
    block = pl.program_id(0)
    inner = x_ref.shape[1]
    bc_width = b_ref.shape[1]
    groups = bc_width // N
    width = inner // groups

    @pl.when(block == 0)
    def _():
        halo = jnp.where(parity_ref[0] == 1, even_ref[...], odd_ref[...])
        x_prev[...] = halo[:, :inner].astype(F32)[8:]
        b_prev[...] = halo[:, inner : inner + bc_width].astype(F32)[8:]
        state[...] = jnp.zeros_like(state)
        decay_product[...] = jnp.ones_like(decay_product)

    raw = raw_ref[...]
    step = jnp.maximum(raw, 0.0) + jnp.log1p(jnp.exp(-jnp.abs(raw)))
    change = -step * jnp.exp(column_of(rate_ref[...]))
    heads = raw.shape[0]
    first = change.astype(BF16)
    rest = change - first.astype(F32)
    second = rest.astype(BF16)
    third = (rest - second.astype(F32)).astype(BF16)
    upper = (
        lax.broadcasted_iota(jnp.int32, (Q, Q), 0) <= lax.broadcasted_iota(jnp.int32, (Q, Q), 1)
    ).astype(F32).astype(BF16)
    sums = jnp.dot(jnp.concatenate([first, second, third], axis=0), upper, preferred_element_type=F32)
    run = sums[:heads] + sums[heads : 2 * heads] + sums[2 * heads :]
    run_ref[...] = run
    shifted_ref[...] = jnp.log(step) - run
    last = run[:, Q - 1 : Q]
    tail = jnp.exp(last - run) * step
    whole = jnp.broadcast_to(jnp.exp(last), (heads, Q))
    columns = pad_rows(jnp.concatenate([*two_terms(tail), *two_terms(whole)], axis=0)).T
    spread = spread_ref[...]
    weight[...] = jnp.dot(columns[:, : 2 * heads].astype(BF16), spread, preferred_element_type=F32)
    decay_row = jnp.dot(
        columns[:16, 2 * heads : 4 * heads].astype(BF16), spread, preferred_element_type=F32
    )[:8]

    bc = conv_rows(b_ref[...].astype(F32), b_prev[...], bt_ref[...].astype(F32))
    b_prev[...] = b_ref[Q - HALO :, :].astype(F32)[8:]
    bc_ref[...] = bc

    def conv_lanes(part, carried):
        lanes = pl.ds(pl.multiple_of(part * LANES, LANES), LANES)
        current = x_ref[:, lanes].astype(F32)
        xc = conv_rows(current, x_prev[:, lanes], xt_ref[:, lanes].astype(F32))
        x_prev[:, lanes] = current[Q - 8 :]
        xc_ref[:, lanes] = xc
        x_weighted[:, lanes] = (xc.astype(F32) * weight[:, lanes]).astype(BF16)
        return carried

    lax.fori_loop(0, inner // LANES, conv_lanes, 0, unroll=16)

    start_ref[...] = decay_product[...]
    decay_product[...] = decay_product[...] * decay_row
    for group in range(groups):
        lanes = slice(group * width, (group + 1) * width)
        fresh = lax.dot_general(
            bc[:, group * N : (group + 1) * N],
            x_weighted[:, lanes],
            (((0,), (0,)), ((), ())),
            preferred_element_type=F32,
        )
        held = state[:, lanes]
        before_ref[:, lanes] = held.astype(BF16)
        state[:, lanes] = held * decay_row[:1, lanes] + fresh

    @pl.when(block == pl.num_programs(0) - 1)
    def _():
        half = inner // 2
        row = lax.broadcasted_iota(jnp.int32, (HALO, half), 0)
        for out_ref, place in ((keep_ref, parity_ref[0]), (send_ref, 1 - parity_ref[0])):
            lanes = pl.ds(pl.multiple_of(place * half, LANES), half)
            out_ref[:N] = state[:, lanes].astype(BF16)
            high, low = two_terms(decay_product[:1, lanes])
            out_ref[N:] = jnp.where(row == 0, high, jnp.where(row == 1, low, 0.0)).astype(BF16)


def local_states(parity, x, b, halos, raw, rate, x_taps, b_taps, spread):
    tokens, inner = x.shape
    bc_width = b.shape[1]
    heads = raw.shape[0]
    blocks = tokens // Q
    half = inner // 2
    whole = lambda c, p: (0, 0)
    rows = lambda c, p: (c, 0)
    columns = lambda c, p: (0, c)
    return pl.pallas_call(
        state_kernel,
        grid_spec=pltpu.PrefetchScalarGridSpec(
            num_scalar_prefetch=1,
            grid=(blocks,),
            in_specs=[
                pl.BlockSpec((Q, inner), rows),
                pl.BlockSpec((Q, bc_width), rows),
                pl.BlockSpec(halos[0].shape, whole),
                pl.BlockSpec(halos[0].shape, whole),
                pl.BlockSpec((heads, Q), columns),
                pl.BlockSpec((1, heads), whole),
                pl.BlockSpec((K, inner), whole),
                pl.BlockSpec((K, bc_width), whole),
                pl.BlockSpec(spread.shape, whole),
            ],
            out_specs=[
                pl.BlockSpec((Q, inner), rows),
                pl.BlockSpec((Q, bc_width), rows),
                pl.BlockSpec((heads, Q), columns),
                pl.BlockSpec((heads, Q), columns),
                pl.BlockSpec((N, inner), rows),
                pl.BlockSpec((8, inner), rows),
                pl.BlockSpec((N + HALO, half), whole),
                pl.BlockSpec((N + HALO, half), whole),
            ],
            scratch_shapes=[
                pltpu.VMEM((8, inner), F32),
                pltpu.VMEM((8, bc_width), F32),
                pltpu.VMEM((Q, inner), F32),
                pltpu.VMEM((Q, inner), BF16),
                pltpu.VMEM((N, inner), F32),
                pltpu.VMEM((8, inner), F32),
            ],
        ),
        out_shape=[
            jax.ShapeDtypeStruct((tokens, inner), BF16),
            jax.ShapeDtypeStruct((tokens, bc_width), BF16),
            jax.ShapeDtypeStruct((heads, tokens), F32),
            jax.ShapeDtypeStruct((heads, tokens), F32),
            jax.ShapeDtypeStruct((blocks * N, inner), BF16),
            jax.ShapeDtypeStruct((blocks * 8, inner), F32),
            jax.ShapeDtypeStruct((N + HALO, half), BF16),
            jax.ShapeDtypeStruct((N + HALO, half), BF16),
        ],
        compiler_params=params(62),
        cost_estimate=cost(150000),
        name="local_states",
    )(parity, x, b, *halos, raw, rate, x_taps, b_taps, spread)


def mix_kernel(
    first, has_alias, parity_ref, *refs
):
    (
        xc_ref, bc_ref, c_ref, c_prev_ref, even_ref, odd_ref, run_ref, shifted_ref, before_ref, start_ref,
        gate_ref, skip_ref, ct_ref, spread_ref,
    ) = refs[:14]
    refs = refs[14 + (3 if has_alias else 0) :]
    part_ref, scale_ref, cc_ref, rise = refs
    block = pl.program_id(0) + first
    inner = xc_ref.shape[1]
    bc_width = c_ref.shape[1]
    groups = bc_width // N
    width = inner // groups
    heads = run_ref.shape[0]

    at = slice(inner + bc_width, inner + 2 * bc_width)
    c_halo = jnp.where(parity_ref[0] == 1, even_ref[:, at], odd_ref[:, at]).astype(F32)[8:]
    c_before = jnp.where(block == 0, c_halo, c_prev_ref[...].astype(F32)[8:])
    cc = conv_rows(c_ref[...].astype(F32), c_before, ct_ref[...].astype(F32))
    cc_ref[...] = cc
    run = run_ref[...]
    columns = pad_rows(jnp.concatenate([*two_terms(jnp.exp(run)), run], axis=0)).T
    rise[...] = jnp.dot(
        columns[:, : 2 * heads].astype(BF16), spread_ref[...], preferred_element_type=F32
    )
    skips = jnp.broadcast_to(jnp.concatenate(two_terms(skip_ref[...]), axis=1), (16, 2 * heads))
    skip = jnp.dot(skips.astype(BF16), spread_ref[...], preferred_element_type=F32)[:1]
    causal = lax.broadcasted_iota(jnp.int32, (Q, Q), 0) >= lax.broadcasted_iota(jnp.int32, (Q, Q), 1)
    left = lax.broadcasted_iota(jnp.int32, (Q, LANES), 1) < P_SIZE
    for group in range(groups):
        state_lanes = slice(group * N, (group + 1) * N)
        scores = lax.dot_general(
            cc[:, state_lanes],
            bc_ref[:, state_lanes],
            (((1,), (1,)), ((), ())),
            preferred_element_type=F32,
        )
        scores = jnp.where(causal, scores, 0.0)
        for pair in range(width // LANES):
            lanes = slice(group * width + pair * LANES, group * width + (pair + 1) * LANES)
            mixing = []
            for head in (lanes.start // P_SIZE, lanes.start // P_SIZE + 1):
                gap = columns[:, 2 * heads + head : 2 * heads + head + 1] + shifted_ref[head : head + 1, :]
                mixing.append((scores * jnp.exp(jnp.where(causal, gap, 0.0))).astype(BF16))
            x = xc_ref[:, lanes].astype(F32)
            x_pair = jnp.concatenate(
                [jnp.where(left, x, 0.0).astype(BF16), jnp.where(left, 0.0, x).astype(BF16)], axis=0
            )
            y = jnp.dot(jnp.concatenate(mixing, axis=1), x_pair, preferred_element_type=F32)
            carried = jnp.dot(cc[:, state_lanes], before_ref[:, lanes], preferred_element_type=F32)
            rise_part = rise[:, lanes]
            y = y + rise_part * carried + skip[:, lanes] * x
            gate = silu(gate_ref[:, lanes].astype(F32))
            part_ref[:, lanes] = (y * gate).astype(BF16)
            scale_ref[:, lanes] = (gate * rise_part * start_ref[:1, lanes]).astype(BF16)


def mix(
    first, count, parity, xc, bc, c, halos, run, shifted, before, start, gate, skip, c_taps, spread, held
):
    tokens, inner = xc.shape
    bc_width = c.shape[1]
    heads = run.shape[0]
    whole = lambda i, p: (0, 0)
    rows = lambda i, p: (first + i, 0)
    columns = lambda i, p: (0, first + i)
    per_block = Q // HALO
    any_spec = pl.BlockSpec(memory_space=pl.ANY)
    aliased = list(held) if held is not None else []
    return pl.pallas_call(
        functools.partial(mix_kernel, first, bool(aliased)),
        grid_spec=pltpu.PrefetchScalarGridSpec(
            num_scalar_prefetch=1,
            grid=(count,),
            in_specs=[
                pl.BlockSpec((Q, inner), rows),
                pl.BlockSpec((Q, bc_width), rows),
                pl.BlockSpec((Q, bc_width), rows),
                pl.BlockSpec(
                    (HALO, bc_width), lambda i, p: (jnp.maximum((first + i) * per_block - 1, 0), 0)
                ),
                pl.BlockSpec(halos[0].shape, whole),
                pl.BlockSpec(halos[0].shape, whole),
                pl.BlockSpec((heads, Q), columns),
                pl.BlockSpec((heads, Q), columns),
                pl.BlockSpec((N, inner), rows),
                pl.BlockSpec((8, inner), rows),
                pl.BlockSpec((Q, inner), rows),
                pl.BlockSpec((1, heads), whole),
                pl.BlockSpec((K, bc_width), whole),
                pl.BlockSpec(spread.shape, whole),
            ]
            + [any_spec] * len(aliased),
            out_specs=[
                pl.BlockSpec((Q, inner), rows),
                pl.BlockSpec((Q, inner), rows),
                pl.BlockSpec((Q, bc_width), rows),
            ],
            scratch_shapes=[pltpu.VMEM((Q, inner), F32)],
        ),
        out_shape=[
            jax.ShapeDtypeStruct((tokens, inner), BF16),
            jax.ShapeDtypeStruct((tokens, inner), BF16),
            jax.ShapeDtypeStruct((tokens, bc_width), BF16),
        ],
        input_output_aliases={15 + i: i for i in range(len(aliased))},
        compiler_params=params(62),
        cost_estimate=cost(count * 25000),
        name="mix",
    )(parity, xc, bc, c, c, *halos, run, shifted, before, start, gate, skip, c_taps, spread, *aliased)


def project_unit(y_ref, w_ref, send_ref, keep_ref, step, units):
    @pl.when(step < units)
    def _():
        send_ref[...] = jnp.dot(y_ref[...], w_ref[...], preferred_element_type=F32).astype(BF16)

    @pl.when(step >= units)
    def _():
        keep_ref[...] = jnp.dot(y_ref[...], w_ref[...], preferred_element_type=F32).astype(BF16)


def norm_kernel(
    tiles, parity_ref, place_ref, part_ref, scale_ref, cc_ref, keep_state_ref, got_ref, gain_ref, w_ref,
    out_ref, send_ref, keep_ref, state,
):
    inner = part_ref.shape[1]
    groups = cc_ref.shape[1] // N
    width = inner // groups
    half = inner // 2
    step = pl.program_id(0)
    tile = part_ref.shape[0]

    @pl.when(step == 0)
    def _():
        for ref, place in ((keep_state_ref, parity_ref[0]), (got_ref, 1 - parity_ref[0])):
            state[:, pl.ds(pl.multiple_of(place * half, LANES), half)] = ref[...]

    @pl.when(step < tiles)
    def _():
        rows = pl.ds(pl.multiple_of(step * tile, tile), tile)
        for group in range(groups):
            lanes = slice(group * width, (group + 1) * width)
            carried = jnp.dot(
                cc_ref[:, group * N : (group + 1) * N], state[:, lanes], preferred_element_type=F32
            )
            gated = part_ref[:, lanes].astype(F32) + scale_ref[:, lanes].astype(F32) * carried
            mean = jnp.sum(gated * gated, axis=1, keepdims=True) * (1.0 / width)
            normed = gated * lax.rsqrt(mean + epsilon) * gain_ref[:, lanes].astype(F32)
            out_ref[rows, lanes] = normed.astype(BF16)

    @pl.when(step >= tiles)
    def _():
        project_unit(out_ref, w_ref, send_ref, keep_ref, step - tiles, pl.num_programs(0) // 2 - tiles // 2)


def norm_project(parity, head, blocks, part, scale, cc, keep, got, gain, weight, width):
    tokens, inner = part.shape
    tile = 2 * Q
    tiles = tokens // tile
    units = len(blocks) // 2
    place = place_of(blocks)
    whole = lambda i, p, q: (0, 0)
    rows = lambda i, p, q: (jnp.minimum(i, tiles - 1), 0)
    return pl.pallas_call(
        functools.partial(norm_kernel, tiles),
        grid_spec=pltpu.PrefetchScalarGridSpec(
            num_scalar_prefetch=2,
            grid=(tiles + 2 * units,),
            in_specs=[
                pl.BlockSpec((tile, inner), rows),
                pl.BlockSpec((tile, inner), rows),
                pl.BlockSpec((tile, cc.shape[1]), rows),
                pl.BlockSpec(keep.shape, whole),
                pl.BlockSpec(got.shape, whole),
                pl.BlockSpec((1, inner), whole),
                pl.BlockSpec((inner, width), lambda i, p, q: (0, place(jnp.maximum(i - tiles, 0), q[0]))),
            ],
            out_specs=[
                pl.BlockSpec((tokens, inner), whole),
                pl.BlockSpec((tokens, width), lambda i, p, q: (0, jnp.clip(i - tiles, 0, units - 1))),
                pl.BlockSpec((tokens, width), lambda i, p, q: (0, jnp.maximum(i - tiles - units, 0))),
            ],
            scratch_shapes=[pltpu.VMEM((N, inner), BF16)],
        ),
        out_shape=[
            jax.ShapeDtypeStruct((tokens, inner), BF16),
            jax.ShapeDtypeStruct((tokens, units * width), BF16),
            jax.ShapeDtypeStruct((tokens, units * width), BF16),
        ],
        compiler_params=params(62),
        cost_estimate=cost(11),
        name="norm_project",
    )(parity, head, part, scale, cc, keep, got, gain, weight)


def add_kernel(left_ref, right_ref, out_ref):
    out_ref[...] = (left_ref[...].astype(F32) + right_ref[...].astype(F32)).astype(BF16)


def add_columns(left, right, first, count, unit):
    tokens = left.shape[0]
    tile = 512
    spec = pl.BlockSpec((tile, unit), lambda i, j: (i, first + j))
    return pl.pallas_call(
        add_kernel,
        grid=(tokens // tile, count),
        in_specs=[spec, spec],
        out_specs=pl.BlockSpec((tile, unit), lambda i, j: (i, j)),
        out_shape=jax.ShapeDtypeStruct((tokens, count * unit), BF16),
        compiler_params=params(62),
        cost_estimate=cost(1),
        name="add_columns",
    )(left, right)


def place_of(blocks):
    def column(step, head):
        column = (head ^ blocks[0][0]) * Y_UNITS + blocks[0][1]
        for index, (bits, unit) in enumerate(blocks[1:], 1):
            column = jnp.where(step == index, (head ^ bits) * Y_UNITS + unit, column)
        return column

    return column


def project_kernel(apart, head_ref, y_ref, w_ref, *outs):
    step = pl.program_id(0)
    if not apart:
        outs[0][...] = jnp.dot(y_ref[...], w_ref[...], preferred_element_type=F32).astype(BF16)
        return
    for unit, out_ref in enumerate(outs):

        @pl.when(step == unit)
        def _(out_ref=out_ref):
            out_ref[...] = jnp.dot(y_ref[...], w_ref[...], preferred_element_type=F32).astype(BF16)


def project(head, blocks, y, weight, width, apart):
    tokens, inner = y.shape
    units = len(blocks)
    place = place_of(blocks)
    if apart:
        out_specs = [pl.BlockSpec((tokens, width), lambda i, p: (0, 0))] * units
        out_shape = [jax.ShapeDtypeStruct((tokens, width), BF16)] * units
    else:
        out_specs = [pl.BlockSpec((tokens, width), lambda i, p: (0, i))]
        out_shape = [jax.ShapeDtypeStruct((tokens, units * width), BF16)]
    return pl.pallas_call(
        functools.partial(project_kernel, apart),
        grid_spec=pltpu.PrefetchScalarGridSpec(
            num_scalar_prefetch=1,
            grid=(units,),
            in_specs=[
                pl.BlockSpec((tokens, inner), lambda i, p: (0, 0)),
                pl.BlockSpec((inner, width), lambda i, p: (0, place(i, p[0]))),
            ],
            out_specs=out_specs,
        ),
        out_shape=out_shape,
        compiler_params=params(62),
        cost_estimate=cost(1),
        name="project",
    )(head, y, weight)


def both_kernel(units, head_ref, y_ref, w_ref, send_ref, keep_ref):
    project_unit(y_ref, w_ref, send_ref, keep_ref, pl.program_id(0), units)


def project_both(head, blocks, y, weight, width):
    tokens, inner = y.shape
    units = len(blocks) // 2
    place = place_of(blocks)
    return pl.pallas_call(
        functools.partial(both_kernel, units),
        grid_spec=pltpu.PrefetchScalarGridSpec(
            num_scalar_prefetch=1,
            grid=(2 * units,),
            in_specs=[
                pl.BlockSpec((tokens, inner), lambda i, p: (0, 0)),
                pl.BlockSpec((inner, width), lambda i, p: (0, place(i, p[0]))),
            ],
            out_specs=[
                pl.BlockSpec((tokens, width), lambda i, p: (0, jnp.minimum(i, units - 1))),
                pl.BlockSpec((tokens, width), lambda i, p: (0, jnp.maximum(i - units, 0))),
            ],
        ),
        out_shape=[jax.ShapeDtypeStruct((tokens, units * width), BF16)] * 2,
        compiler_params=params(62),
        cost_estimate=cost(1),
        name="project_both",
    )(head, y, weight)


def block_slot(block, starts, me, tokens):
    place = me * tokens + block * Q
    slot = 0
    for turn in range(TURN_DEV):
        slot = slot + (starts[TURN_DEV * me + turn] <= place).astype(jnp.int32)
    return slot


def chosen(slot, refs):
    panel = refs[0][...]
    for index in range(1, len(refs)):
        panel = jnp.where(slot == index, refs[index][...], panel)
    return panel


def low_kernel(tokens, start_ref, me_ref, y_ref, *refs):
    panels, out_ref = refs[:-1], refs[-1]
    slot = block_slot(pl.program_id(0), start_ref, me_ref[0], tokens)
    low = lax.dot_general(
        y_ref[...], chosen(slot, panels), (((1,), (1,)), ((), ())), preferred_element_type=F32
    )
    fold = low.shape[0] // 2
    out_ref[...] = jnp.concatenate([low[:fold], low[fold:]], axis=1)


def low_part(starts, me, y, panels):
    tokens, inner = y.shape
    rows = lambda i, s, m: (i, 0)
    whole = lambda i, s, m: (0, 0)
    return pl.pallas_call(
        functools.partial(low_kernel, tokens),
        grid_spec=pltpu.PrefetchScalarGridSpec(
            num_scalar_prefetch=2,
            grid=(tokens // Q,),
            in_specs=[pl.BlockSpec((Q, inner), rows)]
            + [pl.BlockSpec(panel.shape, whole) for panel in panels],
            out_specs=pl.BlockSpec((Q // 2, LANES), rows),
        ),
        out_shape=jax.ShapeDtypeStruct((tokens // 2, LANES), F32),
        compiler_params=params(),
        cost_estimate=cost(4),
        name="low_part",
    )(starts, me, y, *panels)


def held_kernel(counts, unit, *refs):
    own, pair = refs[:Y_UNITS], refs[Y_UNITS : 2 * Y_UNITS]
    parts, out_ref = list(refs[2 * Y_UNITS : -1]), refs[-1]
    for block in range(Y_UNITS):
        total = own[block][...].astype(F32) + pair[block][...].astype(F32)
        for _ in range(counts[block]):
            total = total + parts.pop(0)[...].astype(F32)
        out_ref[:, block * unit : (block + 1) * unit] = total


def held_sum(own, pair, parts, unit):
    tokens = own.shape[0]
    tile = 2 * Q
    column = lambda at: pl.BlockSpec((tile, unit), lambda i: (i, at))
    here = [[(array, at) for array, at, block in parts if block == unit_at] for unit_at in range(Y_UNITS)]
    return pl.pallas_call(
        functools.partial(held_kernel, [len(each) for each in here], unit),
        grid=(tokens // tile,),
        in_specs=[column(block) for block in range(Y_UNITS)]
        + [column(0)] * Y_UNITS
        + [column(at) for each in here for _, at in each],
        out_specs=pl.BlockSpec((tile, Y_UNITS * unit), lambda i: (i, 0)),
        out_shape=jax.ShapeDtypeStruct((tokens, Y_UNITS * unit), F32),
        compiler_params=params(),
        cost_estimate=cost(3),
        name="held_sum",
    )(*[own] * Y_UNITS, *pair, *[array for each in here for array, _ in each])


def final_kernel(tokens, first, unit, start_ref, me_ref, low_ref, held_ref, *refs):
    panels, parts, out_ref = refs[: TURN_DEV + 1], refs[TURN_DEV + 1 : -1], refs[-1]
    rank = LANES // 2
    slot = block_slot(pl.program_id(0), start_ref, me_ref[0], tokens)
    low = low_ref[...].astype(BF16)
    low = jnp.concatenate([low[:, :rank], low[:, rank:]], axis=0)
    total = held_ref[...] + jnp.dot(low, chosen(slot, panels), preferred_element_type=F32)
    start = first * unit
    out_ref[:, :start] = total[:, :start].astype(BF16)
    rest = total[:, start:]
    for part in parts:
        rest = rest + part[...].astype(F32)
    out_ref[:, start:] = rest.astype(BF16)


def final_sum(starts, me, low, held, panels, parts, first, unit):
    tokens, features = held.shape
    rows = lambda i, s, m: (i, 0)
    whole = lambda i, s, m: (0, 0)
    return pl.pallas_call(
        functools.partial(final_kernel, tokens, first, unit),
        grid_spec=pltpu.PrefetchScalarGridSpec(
            num_scalar_prefetch=2,
            grid=(tokens // Q,),
            in_specs=[pl.BlockSpec((Q // 2, LANES), rows), pl.BlockSpec((Q, features), rows)]
            + [pl.BlockSpec(panel.shape, whole) for panel in panels]
            + [pl.BlockSpec((Q, part.shape[1]), rows) for part in parts],
            out_specs=pl.BlockSpec((Q, features), rows),
        ),
        out_shape=jax.ShapeDtypeStruct((tokens, features), BF16),
        compiler_params=params(),
        cost_estimate=cost(3),
        name="final_sum",
    )(starts, me, low, held, *panels, *parts)


def shift_up(block, axis, distance):
    devices = range(lax.axis_size(axis))
    route = [(i, i + distance) for i in devices if i + distance in devices]
    return lax.ppermute(block, axis, route)


def swap(block, axis, bits):
    return lax.ppermute(block, axis, [(i, i ^ bits) for i in range(lax.axis_size(axis))])


def after(value, *earlier):
    return lax.optimization_barrier((value, *earlier))[0]


def neighbour_edge(edge):
    size = lax.axis_size("ctx")
    even = lax.ppermute(edge, "ctx", [(i, i ^ 1) for i in range(size)])
    odd = lax.ppermute(edge, "ctx", [(i, i + 1 if i % 2 else i - 1) for i in range(1, size - 1)])
    return even, odd


class Route:
    def __init__(self, bits, send, keep):
        self.bits, self.send, self.keep = list(bits), send, keep
        self.got = None

    def merge(self, *earlier):
        half = self.keep.shape[0] // 2
        got = after(self.got, *earlier) if earlier else self.got
        self.send = self.keep[:half] + got[:half]
        self.keep = self.keep[half:] + got[half:]
        self.got = None
        return self.send

    def step(self, *earlier):
        if not self.bits:
            return
        if self.got is not None:
            self.merge(*earlier)
        send = after(self.send, *earlier) if earlier else self.send
        self.got = swap(send, "ctx", self.bits.pop(0))

    def end(self, *earlier):
        while self.bits:
            self.step(*earlier)
        keep, got = self.keep, self.got
        if earlier:
            keep = after(keep, *earlier)
        return keep[0] + got[0]


def unpacked(packed):
    decay = packed[N : N + 1].astype(F32) + packed[N + 1 : N + 2].astype(F32)
    return packed[:N].astype(F32), decay


def packed(state, decay):
    high = decay.astype(BF16)
    low = (decay - high.astype(F32)).astype(BF16)
    fill = jnp.zeros((HALO - 2, state.shape[1]), BF16)
    return jnp.concatenate([state.astype(BF16), high, low, fill], axis=0)


def local(
    input_x_channels,
    input_b_channels,
    input_c_channels,
    input_gate_channels,
    raw_step_sizes,
    log_decay_rate,
    head_skip_coeff,
    x_conv_taps,
    b_conv_taps,
    c_conv_taps,
    gated_norm_gain,
    output_weight,
    adapter_down_panels,
    adapter_up_panels,
    turn_first_token,
    tenant_of_turn,
    tenant_panel_index,
):
    tokens, inner = input_x_channels.shape
    heads = log_decay_rate.shape[0]
    blocks = tokens // Q
    features = adapter_up_panels.shape[2]
    unit = features // Y_UNITS
    ctx = lax.axis_index("ctx").astype(jnp.int32)
    head = lax.axis_index("head").astype(jnp.int32)
    devices = lax.axis_size("ctx")
    parity = ctx % 2
    first = parity == 0
    me = ctx[None]
    parity_arg, head_arg = parity[None], head[None]
    down = jnp.swapaxes(adapter_down_panels, 1, 2)
    up = adapter_up_panels
    outer = [1 << bit for bit in range(1, devices.bit_length() - 1)]
    near, far = [1] + outer, outer + [1]

    edge = sequence_edge(input_x_channels, input_b_channels, input_c_channels)
    halos = neighbour_edge(edge)

    slots = range(TURN_DEV)
    packs = pack_panels(
        [(down, near, slots[1:]), (down, far, slots[:1]), (up, near, slots)],
        tenant_panel_index, tenant_of_turn, me, devices,
    )
    down_late, down_early, ups = [
        Route(bits, *pack) for bits, pack in zip((near, far, near), packs)
    ]
    down_late.step()
    down_early.step()

    lane_head = jnp.arange(inner) // P_SIZE
    spread = (jnp.arange(2 * heads)[:, None] % heads == lane_head[None, :]).astype(BF16)
    xc, bc, run, shifted, before, start, keep, send = local_states(
        after(parity_arg, packs[0][0]),
        input_x_channels,
        input_b_channels,
        halos,
        raw_step_sizes,
        log_decay_rate[None],
        x_conv_taps,
        b_conv_taps,
        spread,
    )
    count = blocks // PIECES

    def mix_piece(piece, held, *earlier):
        return mix(
            piece * count, count, after(parity_arg, *earlier), xc, bc, input_c_channels, halos, run, shifted,
            before, start, input_gate_channels, head_skip_coeff[None], c_conv_taps, spread, held,
        )

    got = swap(send, "ctx", 1)
    held = mix_piece(0, None, send)
    got = after(got, held[2])
    own_state, own_decay = unpacked(keep)
    got_state, got_decay = unpacked(got)
    first_state = jnp.where(first, own_state, got_state)
    first_decay = jnp.where(first, own_decay, got_decay)
    total = jnp.where(first, got_state, own_state)
    total_decay = jnp.where(first, got_decay, own_decay)
    total, total_decay = total + total_decay * first_state, total_decay * first_decay
    early = [down_late.got, down_early.got]
    ups.step(got)
    incoming = jnp.zeros_like(total)
    incoming_decay = jnp.ones_like(total_decay)
    piece = 1
    for bit in outer:
        sent = packed(total, total_decay)
        got = swap(sent, "ctx", bit)
        if piece < PIECES - 1:
            held = mix_piece(piece, held, sent, *early)
            merged = [held[2]]
            if bit == outer[-1]:
                merged += [route.merge(sent) for route in (down_late, down_early)]
            got = after(got, *merged)
            piece += 1
        state, decay = unpacked(got)
        upper = (ctx & bit) != 0
        incoming = jnp.where(upper, incoming + incoming_decay * state, incoming)
        incoming_decay = jnp.where(upper, incoming_decay * decay, incoming_decay)
        total, total_decay = (
            jnp.where(upper, total + total_decay * state, state + decay * total),
            total_decay * decay,
        )
    incoming_second = first_state + first_decay * incoming
    back_sent = jnp.where(first, incoming_second, incoming).astype(BF16)
    kept = jnp.where(first, incoming, incoming_second).astype(BF16)
    back = swap(back_sent, "ctx", 1)
    for route in (down_late, down_early):
        route.step(back_sent)
    while piece < PIECES:
        held = mix_piece(piece, held, back_sent, ups.got)
        piece += 1
    part, scale, cc = held

    chips = range(1, lax.axis_size("head") // 2)
    first, later = range(Y_FIRST), range(Y_FIRST, Y_UNITS)

    def sides(units):
        return [(2 * chip ^ core, at) for core in (1, 0) for chip in chips for at in units]

    parts = []

    def send_both(mine, to_pair, units, *earlier):
        from_pair = swap(after(to_pair, *earlier), "head", 1)
        sums = []
        for chip in chips:
            both = add_columns(mine, from_pair, (chip - 1) * len(units), len(units), unit)
            arrived = swap(both, "head", 2 * chip)
            parts.extend((arrived, at - units.start, at) for at in units)
            sums.append(both)
        return sums

    routes = (down_late, down_early, ups)
    y_normed, to_pair, mine = norm_project(
        parity_arg, head_arg, sides(first), part, scale, cc, kept, back,
        gated_norm_gain[None], output_weight, unit,
    )
    sums = send_both(mine, to_pair, first, *[route.got for route in routes])
    for route in routes:
        route.step(*sums)
    to_pair, mine = project_both(after(head_arg, *sums), sides(later), y_normed, output_weight, unit)
    sums = send_both(
        mine, to_pair, later, *[arrived for arrived, _, _ in parts], *[route.got for route in routes]
    )
    down_second = down_late.end(*sums)
    down_first = down_early.end(*sums)
    down_before = shift_up(down_second, "ctx", 1)
    ups.step(*sums)
    to_pair = project(
        after(head_arg, *sums), [(1, at) for at in range(Y_UNITS)], y_normed, output_weight, unit, True
    )
    pair = [swap(each, "head", 1) for each in to_pair]
    (own,) = project(
        after(head_arg, *to_pair, down_before, ups.got),
        [(0, at) for at in range(Y_UNITS)], y_normed, output_weight, unit, False,
    )
    up_own = ups.end(*to_pair)
    rank = up.shape[1]
    up_first, up_second = up_own[:rank], up_own[rank:]
    up_before = shift_up(up_second, "ctx", 1)
    low = low_part(
        after(turn_first_token, own, up_before), me, y_normed, [down_before, down_first, down_second]
    )
    low = low + swap(low, "head", 1)
    low_sent = low.astype(BF16)
    for chip in chips:
        low = low + swap(low_sent, "head", 2 * chip).astype(F32)
    here = [each for each in parts if each[2] in first]
    held = held_sum(own, pair, here, unit)
    last = [arrived for arrived, at, _ in parts[len(here) :] if at == 0]
    return final_sum(
        turn_first_token, me, low, held, [up_before, up_first, up_second], last, Y_FIRST, unit
    )


def solution(mesh):
    in_specs = (
        P("ctx", "head"),
        P("ctx", "head"),
        P("ctx", "head"),
        P("ctx", "head"),
        P("head", "ctx"),
        P("head"),
        P("head"),
        P(None, "head"),
        P(None, "head"),
        P(None, "head"),
        P("head"),
        P("head", None),
        P("ctx", "head", None),
        P("ctx", None, "head"),
        P(),
        P(),
        P(),
    )
    out_specs = P("ctx", "head")
    return jax.shard_map(local, mesh=mesh, in_specs=in_specs, out_specs=out_specs, check_vma=False)
```

```python
import functools

import jax
import jax.numpy as jnp
import ml_dtypes
import numpy as np
from jax import lax
from jax.experimental import pallas as pl
from jax.experimental.pallas import tpu as pltpu
from jax.sharding import PartitionSpec as P

P_SIZE = 64
N = 128
K = 4
Q = 128
TURN_DEV = 2
HALO = 16
LANES = 128
PIECES = 2
STATE_BLOCKS = 2
FINAL_BLOCKS = 2
Y_UNITS = 4
Y_FIRST = 2

F32 = jnp.float32
BF16 = jnp.bfloat16
epsilon = 1e-05
MIB = 1024 * 1024


def params(mib=28):
    return pltpu.CompilerParams(vmem_limit_bytes=mib * MIB)


def cost(microseconds):
    return pl.CostEstimate(flops=int(microseconds * 1e5), bytes_accessed=1, transcendentals=0)


def silu(v):
    half = 0.5 * v
    return half + half * jnp.tanh(half)


def conv_rows(current, previous, taps):
    rows = current.shape[0]
    joined = jnp.concatenate([previous, current], axis=0)
    total = taps[K - 1 : K] * current
    for back in range(1, K):
        total = total + taps[K - 1 - back : K - back] * pltpu.roll(joined, back, 0)[8 : 8 + rows]
    return silu(total).astype(BF16)


def two_terms(v):
    high = v.astype(BF16).astype(F32)
    return high, v - high


def column_of(row):
    size = row.shape[1]
    here = lax.broadcasted_iota(jnp.int32, (size, size), 0)
    there = lax.broadcasted_iota(jnp.int32, (size, size), 1)
    return jnp.sum(jnp.where(here == there, row, 0.0), axis=1, keepdims=True)


def pad_rows(stack):
    rows = stack.shape[0]
    if rows % LANES:
        fill = jnp.zeros((LANES - rows % LANES, stack.shape[1]), F32)
        stack = jnp.concatenate([stack, fill], axis=0)
    return stack


def edge_kernel(x_ref, b_ref, c_ref, out_ref):
    place = 0
    for ref in (x_ref, b_ref, c_ref):
        out_ref[:, place : place + ref.shape[1]] = ref[...]
        place += ref.shape[1]


def sequence_edge(*arrays):
    tokens = arrays[0].shape[0]
    width = sum(array.shape[1] for array in arrays)
    return pl.pallas_call(
        edge_kernel,
        grid=(1,),
        in_specs=[
            pl.BlockSpec((HALO, array.shape[1]), lambda i: (tokens // HALO - 1, 0)) for array in arrays
        ],
        out_specs=pl.BlockSpec((HALO, width), lambda i: (0, 0)),
        out_shape=jax.ShapeDtypeStruct((HALO, width), BF16),
        compiler_params=params(62),
        cost_estimate=cost(1),
        name="sequence_edge",
    )(*arrays)


def panel_home(place, panel_index, tenants, me, *, bits, slot, count):
    relative = 0
    for order, bit in enumerate(bits):
        relative += bit * (1 - (place >> (len(bits) - 1 - order)) % 2)
    panel = panel_index[tenants[TURN_DEV * (relative ^ me) + slot]]
    owned = lax.div(panel, count) == me
    return jnp.where(owned, lax.rem(panel, count), 0), owned


def panel_kernel(homes, devices, index_ref, tenant_ref, me_ref, *refs):
    ins, outs = refs[: len(homes)], refs[len(homes) : 3 * len(homes)]
    zeros, sems = refs[-2:]
    zeros[...] = jnp.zeros_like(zeros)
    half = devices // 2
    started = []
    for number, job in enumerate(homes):
        in_ref = ins[number]
        rows, width = in_ref.shape[1:]
        for place in range(devices):
            out_ref = outs[2 * number + (place >= half)]
            for slot, home in enumerate(job):
                local, owned = home(place, index_ref, tenant_ref, me_ref[0])
                out = out_ref.at[place % half, pl.ds(slot * rows, rows), :]
                sem = sems.at[len(started)]
                own = pltpu.make_async_copy(in_ref.at[local], out, sem)
                none = pltpu.make_async_copy(zeros.at[pl.ds(0, rows), pl.ds(0, width)], out, sem)

                @pl.when(owned)
                def _(own=own):
                    own.start()

                @pl.when(jnp.logical_not(owned))
                def _(none=none):
                    none.start()

                started.append(none)
    for copy in started:
        copy.wait()


def pack_panels(jobs, panel_index, tenants, me, devices):
    half = devices // 2
    homes, out_shape, copies = [], [], 0
    for panels, bits, slots in jobs:
        count, rows, width = panels.shape
        homes.append(
            [
                functools.partial(panel_home, bits=bits, slot=slot, count=count)
                for slot in slots
            ]
        )
        out_shape += [jax.ShapeDtypeStruct((half, len(slots) * rows, width), BF16)] * 2
        copies += devices * len(slots)
    zero_shape = tuple(max(panels.shape[axis] for panels, _, _ in jobs) for axis in (1, 2))
    outs = pl.pallas_call(
        functools.partial(panel_kernel, homes, devices),
        grid_spec=pltpu.PrefetchScalarGridSpec(
            num_scalar_prefetch=3,
            grid=(1,),
            in_specs=[pl.BlockSpec(job[0].shape, lambda i, *_: (0, 0, 0)) for job in jobs],
            out_specs=[pl.BlockSpec(memory_space=pl.ANY)] * len(out_shape),
            scratch_shapes=[pltpu.VMEM(zero_shape, BF16), pltpu.SemaphoreType.DMA((copies,))],
        ),
        out_shape=out_shape,
        compiler_params=params(62),
        cost_estimate=cost(5),
        name="pack_panels",
    )(panel_index, tenants, me, *[job[0] for job in jobs])
    return [outs[2 * job : 2 * job + 2] for job in range(len(jobs))]


def state_kernel(
    parity_ref, x_ref, b_ref, even_ref, odd_ref, raw_ref, rate_ref, xt_ref, bt_ref, spread_ref,
    xc_ref, bc_ref, run_ref, shifted_ref, before_ref, start_ref, keep_ref, send_ref,
    x_prev, b_prev, weight, x_weighted, state, decay_product,
):
    block = pl.program_id(0)
    inner = x_ref.shape[1]
    bc_width = b_ref.shape[1]
    groups = bc_width // N
    width = inner // groups

    @pl.when(block == 0)
    def _():
        halo = jnp.where(parity_ref[0] == 1, even_ref[...], odd_ref[...])
        x_prev[...] = halo[:, :inner].astype(F32)[8:]
        b_prev[...] = halo[:, inner : inner + bc_width].astype(F32)[8:]
        state[...] = jnp.zeros_like(state)
        decay_product[...] = jnp.ones_like(decay_product)

    raw = raw_ref[...]
    step = jnp.maximum(raw, 0.0) + jnp.log1p(jnp.exp(-jnp.abs(raw)))
    change = -step * jnp.exp(column_of(rate_ref[...]))
    heads = raw.shape[0]
    first = change.astype(BF16)
    rest = change - first.astype(F32)
    second = rest.astype(BF16)
    third = (rest - second.astype(F32)).astype(BF16)
    terms = jnp.concatenate([first, second, third], axis=0)
    upper = (
        lax.broadcasted_iota(jnp.int32, (Q, Q), 0) <= lax.broadcasted_iota(jnp.int32, (Q, Q), 1)
    ).astype(F32).astype(BF16)
    spread = spread_ref[...]
    parts = [slice(part * Q, (part + 1) * Q) for part in range(STATE_BLOCKS)]
    decay_rows = []
    for rows in parts:
        sums = jnp.dot(terms[:, rows], upper, preferred_element_type=F32)
        run = sums[:heads] + sums[heads : 2 * heads] + sums[2 * heads :]
        run_ref[:, rows] = run
        shifted_ref[:, rows] = jnp.log(step[:, rows]) - run
        last = run[:, Q - 1 : Q]
        tail = jnp.exp(last - run) * step[:, rows]
        whole = jnp.broadcast_to(jnp.exp(last), (heads, Q))
        columns = pad_rows(jnp.concatenate([*two_terms(tail), *two_terms(whole)], axis=0)).T
        weight[rows, :] = jnp.dot(
            columns[:, : 2 * heads].astype(BF16), spread, preferred_element_type=F32
        )
        decay_rows.append(
            jnp.dot(columns[:16, 2 * heads : 4 * heads].astype(BF16), spread, preferred_element_type=F32)[:8]
        )

    bc = conv_rows(b_ref[...].astype(F32), b_prev[...], bt_ref[...].astype(F32))
    b_prev[...] = b_ref[STATE_BLOCKS * Q - HALO :, :].astype(F32)[8:]
    bc_ref[...] = bc

    def conv_lanes(part, carried):
        lanes = pl.ds(pl.multiple_of(part * LANES, LANES), LANES)
        current = x_ref[:, lanes].astype(F32)
        xc = conv_rows(current, x_prev[:, lanes], xt_ref[:, lanes].astype(F32))
        x_prev[:, lanes] = current[STATE_BLOCKS * Q - 8 :]
        xc_ref[:, lanes] = xc
        x_weighted[:, lanes] = (xc.astype(F32) * weight[:, lanes]).astype(BF16)
        return carried

    lax.fori_loop(0, inner // LANES, conv_lanes, 0, unroll=16)

    for part, (rows, decay_row) in enumerate(zip(parts, decay_rows)):
        start_ref[part * 8 : (part + 1) * 8, :] = decay_product[...]
        decay_product[...] = decay_product[...] * decay_row
        for group in range(groups):
            lanes = slice(group * width, (group + 1) * width)
            fresh = lax.dot_general(
                bc[rows, group * N : (group + 1) * N],
                x_weighted[rows, lanes],
                (((0,), (0,)), ((), ())),
                preferred_element_type=F32,
            )
            held = state[:, lanes]
            before_ref[part * N : (part + 1) * N, lanes] = held.astype(BF16)
            state[:, lanes] = held * decay_row[:1, lanes] + fresh

    @pl.when(block == pl.num_programs(0) - 1)
    def _():
        half = inner // 2
        row = lax.broadcasted_iota(jnp.int32, (HALO, half), 0)
        for out_ref, place in ((keep_ref, parity_ref[0]), (send_ref, 1 - parity_ref[0])):
            lanes = pl.ds(pl.multiple_of(place * half, LANES), half)
            out_ref[:N] = state[:, lanes].astype(BF16)
            high, low = two_terms(decay_product[:1, lanes])
            out_ref[N:] = jnp.where(row == 0, high, jnp.where(row == 1, low, 0.0)).astype(BF16)


def local_states(parity, x, b, halos, raw, rate, x_taps, b_taps, spread):
    tokens, inner = x.shape
    bc_width = b.shape[1]
    heads = raw.shape[0]
    blocks = tokens // Q
    half = inner // 2
    span = STATE_BLOCKS * Q
    whole = lambda c, p: (0, 0)
    rows = lambda c, p: (c, 0)
    columns = lambda c, p: (0, c)
    return pl.pallas_call(
        state_kernel,
        grid_spec=pltpu.PrefetchScalarGridSpec(
            num_scalar_prefetch=1,
            grid=(blocks // STATE_BLOCKS,),
            in_specs=[
                pl.BlockSpec((span, inner), rows),
                pl.BlockSpec((span, bc_width), rows),
                pl.BlockSpec(halos[0].shape, whole),
                pl.BlockSpec(halos[0].shape, whole),
                pl.BlockSpec((heads, span), columns),
                pl.BlockSpec((1, heads), whole),
                pl.BlockSpec((K, inner), whole),
                pl.BlockSpec((K, bc_width), whole),
                pl.BlockSpec(spread.shape, whole),
            ],
            out_specs=[
                pl.BlockSpec((span, inner), rows),
                pl.BlockSpec((span, bc_width), rows),
                pl.BlockSpec((heads, span), columns),
                pl.BlockSpec((heads, span), columns),
                pl.BlockSpec((STATE_BLOCKS * N, inner), rows),
                pl.BlockSpec((STATE_BLOCKS * 8, inner), rows),
                pl.BlockSpec((N + HALO, half), whole),
                pl.BlockSpec((N + HALO, half), whole),
            ],
            scratch_shapes=[
                pltpu.VMEM((8, inner), F32),
                pltpu.VMEM((8, bc_width), F32),
                pltpu.VMEM((span, inner), F32),
                pltpu.VMEM((span, inner), BF16),
                pltpu.VMEM((N, inner), F32),
                pltpu.VMEM((8, inner), F32),
            ],
        ),
        out_shape=[
            jax.ShapeDtypeStruct((tokens, inner), BF16),
            jax.ShapeDtypeStruct((tokens, bc_width), BF16),
            jax.ShapeDtypeStruct((heads, tokens), F32),
            jax.ShapeDtypeStruct((heads, tokens), F32),
            jax.ShapeDtypeStruct((blocks * N, inner), BF16),
            jax.ShapeDtypeStruct((blocks * 8, inner), F32),
            jax.ShapeDtypeStruct((N + HALO, half), BF16),
            jax.ShapeDtypeStruct((N + HALO, half), BF16),
        ],
        compiler_params=params(62),
        cost_estimate=cost(150000),
        name="local_states",
    )(parity, x, b, *halos, raw, rate, x_taps, b_taps, spread)


def mix_kernel(
    first, has_alias, parity_ref, *refs
):
    (
        xc_ref, bc_ref, c_ref, c_prev_ref, even_ref, odd_ref, run_ref, shifted_ref, before_ref, start_ref,
        gate_ref, skip_ref, ct_ref, spread_ref,
    ) = refs[:14]
    refs = refs[14 + (3 if has_alias else 0) :]
    part_ref, scale_ref, cc_ref, rise = refs
    block = pl.program_id(0) + first
    inner = xc_ref.shape[1]
    bc_width = c_ref.shape[1]
    groups = bc_width // N
    width = inner // groups
    heads = run_ref.shape[0]

    at = slice(inner + bc_width, inner + 2 * bc_width)
    c_halo = jnp.where(parity_ref[0] == 1, even_ref[:, at], odd_ref[:, at]).astype(F32)[8:]
    c_before = jnp.where(block == 0, c_halo, c_prev_ref[...].astype(F32)[8:])
    cc = conv_rows(c_ref[...].astype(F32), c_before, ct_ref[...].astype(F32))
    cc_ref[...] = cc
    run = run_ref[...]
    columns = pad_rows(jnp.concatenate([*two_terms(jnp.exp(run)), run], axis=0)).T
    rise[...] = jnp.dot(
        columns[:, : 2 * heads].astype(BF16), spread_ref[...], preferred_element_type=F32
    )
    skips = jnp.broadcast_to(jnp.concatenate(two_terms(skip_ref[...]), axis=1), (16, 2 * heads))
    skip = jnp.dot(skips.astype(BF16), spread_ref[...], preferred_element_type=F32)[:1]
    causal = lax.broadcasted_iota(jnp.int32, (Q, Q), 0) >= lax.broadcasted_iota(jnp.int32, (Q, Q), 1)
    left = lax.broadcasted_iota(jnp.int32, (Q, LANES), 1) < P_SIZE
    for group in range(groups):
        state_lanes = slice(group * N, (group + 1) * N)
        scores = lax.dot_general(
            cc[:, state_lanes],
            bc_ref[:, state_lanes],
            (((1,), (1,)), ((), ())),
            preferred_element_type=F32,
        )
        scores = jnp.where(causal, scores, 0.0)
        for pair in range(width // LANES):
            lanes = slice(group * width + pair * LANES, group * width + (pair + 1) * LANES)
            mixing = []
            for head in (lanes.start // P_SIZE, lanes.start // P_SIZE + 1):
                gap = columns[:, 2 * heads + head : 2 * heads + head + 1] + shifted_ref[head : head + 1, :]
                mixing.append((scores * jnp.exp(jnp.where(causal, gap, 0.0))).astype(BF16))
            x = xc_ref[:, lanes].astype(F32)
            x_pair = jnp.concatenate(
                [jnp.where(left, x, 0.0).astype(BF16), jnp.where(left, 0.0, x).astype(BF16)], axis=0
            )
            y = jnp.dot(jnp.concatenate(mixing, axis=1), x_pair, preferred_element_type=F32)
            carried = jnp.dot(cc[:, state_lanes], before_ref[:, lanes], preferred_element_type=F32)
            rise_part = rise[:, lanes]
            y = y + rise_part * carried + skip[:, lanes] * x
            gate = silu(gate_ref[:, lanes].astype(F32))
            part_ref[:, lanes] = (y * gate).astype(BF16)
            scale_ref[:, lanes] = (gate * rise_part * start_ref[:1, lanes]).astype(BF16)


def mix(
    first, count, parity, xc, bc, c, halos, run, shifted, before, start, gate, skip, c_taps, spread, held
):
    tokens, inner = xc.shape
    bc_width = c.shape[1]
    heads = run.shape[0]
    whole = lambda i, p: (0, 0)
    rows = lambda i, p: (first + i, 0)
    columns = lambda i, p: (0, first + i)
    per_block = Q // HALO
    any_spec = pl.BlockSpec(memory_space=pl.ANY)
    aliased = list(held) if held is not None else []
    return pl.pallas_call(
        functools.partial(mix_kernel, first, bool(aliased)),
        grid_spec=pltpu.PrefetchScalarGridSpec(
            num_scalar_prefetch=1,
            grid=(count,),
            in_specs=[
                pl.BlockSpec((Q, inner), rows),
                pl.BlockSpec((Q, bc_width), rows),
                pl.BlockSpec((Q, bc_width), rows),
                pl.BlockSpec(
                    (HALO, bc_width), lambda i, p: (jnp.maximum((first + i) * per_block - 1, 0), 0)
                ),
                pl.BlockSpec(halos[0].shape, whole),
                pl.BlockSpec(halos[0].shape, whole),
                pl.BlockSpec((heads, Q), columns),
                pl.BlockSpec((heads, Q), columns),
                pl.BlockSpec((N, inner), rows),
                pl.BlockSpec((8, inner), rows),
                pl.BlockSpec((Q, inner), rows),
                pl.BlockSpec((1, heads), whole),
                pl.BlockSpec((K, bc_width), whole),
                pl.BlockSpec(spread.shape, whole),
            ]
            + [any_spec] * len(aliased),
            out_specs=[
                pl.BlockSpec((Q, inner), rows),
                pl.BlockSpec((Q, inner), rows),
                pl.BlockSpec((Q, bc_width), rows),
            ],
            scratch_shapes=[pltpu.VMEM((Q, inner), F32)],
        ),
        out_shape=[
            jax.ShapeDtypeStruct((tokens, inner), BF16),
            jax.ShapeDtypeStruct((tokens, inner), BF16),
            jax.ShapeDtypeStruct((tokens, bc_width), BF16),
        ],
        input_output_aliases={15 + i: i for i in range(len(aliased))},
        compiler_params=params(62),
        cost_estimate=cost(count * 25000),
        name="mix",
    )(parity, xc, bc, c, c, *halos, run, shifted, before, start, gate, skip, c_taps, spread, *aliased)


def project_unit(y_ref, w_ref, send_ref, keep_ref, step, units):
    @pl.when(step < units)
    def _():
        send_ref[...] = jnp.dot(y_ref[...], w_ref[...], preferred_element_type=F32).astype(BF16)

    @pl.when(step >= units)
    def _():
        keep_ref[...] = jnp.dot(y_ref[...], w_ref[...], preferred_element_type=F32).astype(BF16)


def norm_kernel(
    tiles, parity_ref, place_ref, part_ref, scale_ref, cc_ref, keep_state_ref, got_ref, gain_ref, w_ref,
    out_ref, send_ref, keep_ref, state,
):
    inner = part_ref.shape[1]
    groups = cc_ref.shape[1] // N
    width = inner // groups
    half = inner // 2
    step = pl.program_id(0)
    tile = part_ref.shape[0]

    @pl.when(step == 0)
    def _():
        for ref, place in ((keep_state_ref, parity_ref[0]), (got_ref, 1 - parity_ref[0])):
            state[:, pl.ds(pl.multiple_of(place * half, LANES), half)] = ref[...]

    @pl.when(step < tiles)
    def _():
        rows = pl.ds(pl.multiple_of(step * tile, tile), tile)
        for group in range(groups):
            lanes = slice(group * width, (group + 1) * width)
            carried = jnp.dot(
                cc_ref[:, group * N : (group + 1) * N], state[:, lanes], preferred_element_type=F32
            )
            gated = part_ref[:, lanes].astype(F32) + scale_ref[:, lanes].astype(F32) * carried
            mean = jnp.sum(gated * gated, axis=1, keepdims=True) * (1.0 / width)
            normed = gated * lax.rsqrt(mean + epsilon) * gain_ref[:, lanes].astype(F32)
            out_ref[rows, lanes] = normed.astype(BF16)

    @pl.when(step >= tiles)
    def _():
        project_unit(out_ref, w_ref, send_ref, keep_ref, step - tiles, pl.num_programs(0) // 2 - tiles // 2)


def norm_project(parity, head, blocks, part, scale, cc, keep, got, gain, weight, width):
    tokens, inner = part.shape
    tile = 2 * Q
    tiles = tokens // tile
    units = len(blocks) // 2
    place = place_of(blocks)
    whole = lambda i, p, q: (0, 0)
    rows = lambda i, p, q: (jnp.minimum(i, tiles - 1), 0)
    return pl.pallas_call(
        functools.partial(norm_kernel, tiles),
        grid_spec=pltpu.PrefetchScalarGridSpec(
            num_scalar_prefetch=2,
            grid=(tiles + 2 * units,),
            in_specs=[
                pl.BlockSpec((tile, inner), rows),
                pl.BlockSpec((tile, inner), rows),
                pl.BlockSpec((tile, cc.shape[1]), rows),
                pl.BlockSpec(keep.shape, whole),
                pl.BlockSpec(got.shape, whole),
                pl.BlockSpec((1, inner), whole),
                pl.BlockSpec((inner, width), lambda i, p, q: (0, place(jnp.maximum(i - tiles, 0), q[0]))),
            ],
            out_specs=[
                pl.BlockSpec((tokens, inner), whole),
                pl.BlockSpec((tokens, width), lambda i, p, q: (0, jnp.clip(i - tiles, 0, units - 1))),
                pl.BlockSpec((tokens, width), lambda i, p, q: (0, jnp.maximum(i - tiles - units, 0))),
            ],
            scratch_shapes=[pltpu.VMEM((N, inner), BF16)],
        ),
        out_shape=[
            jax.ShapeDtypeStruct((tokens, inner), BF16),
            jax.ShapeDtypeStruct((tokens, units * width), BF16),
            jax.ShapeDtypeStruct((tokens, units * width), BF16),
        ],
        compiler_params=params(62),
        cost_estimate=cost(11),
        name="norm_project",
    )(parity, head, part, scale, cc, keep, got, gain, weight)


def place_of(blocks):
    def column(step, head):
        column = (head ^ blocks[0][0]) * Y_UNITS + blocks[0][1]
        for index, (bits, unit) in enumerate(blocks[1:], 1):
            column = jnp.where(step == index, (head ^ bits) * Y_UNITS + unit, column)
        return column

    return column


def rest_kernel(counts, head_ref, y_ref, w_ref, *outs):
    step = pl.program_id(0)
    start = 0
    for count, out_ref in zip(counts, outs):

        @pl.when((step >= start) & (step < start + count))
        def _(out_ref=out_ref):
            out_ref[...] = jnp.dot(y_ref[...], w_ref[...], preferred_element_type=F32).astype(BF16)

        start += count


def project_rest(head, sides, y, weight, width, microseconds):
    tokens, inner = y.shape
    counts = [len(side) for side in sides]
    blocks = [block for side in sides for block in side]
    place = place_of(blocks)
    out_specs, start = [], 0
    for count in counts:
        out_specs.append(
            pl.BlockSpec(
                (tokens, width),
                lambda i, p, start=start, count=count: (0, jnp.clip(i - start, 0, count - 1)),
            )
        )
        start += count
    return pl.pallas_call(
        functools.partial(rest_kernel, counts),
        grid_spec=pltpu.PrefetchScalarGridSpec(
            num_scalar_prefetch=1,
            grid=(len(blocks),),
            in_specs=[
                pl.BlockSpec((tokens, inner), lambda i, p: (0, 0)),
                pl.BlockSpec((inner, width), lambda i, p: (0, place(i, p[0]))),
            ],
            out_specs=out_specs,
        ),
        out_shape=[jax.ShapeDtypeStruct((tokens, count * width), BF16) for count in counts],
        compiler_params=params(62),
        cost_estimate=cost(microseconds),
        name="project_rest",
    )(head, y, weight)


def block_slot(block, starts, me, tokens):
    place = me * tokens + block * Q
    slot = 0
    for turn in range(TURN_DEV):
        slot = slot + (starts[TURN_DEV * me + turn] <= place).astype(jnp.int32)
    return slot


def chosen(slot, refs):
    panel = refs[0][...]
    for index in range(1, len(refs)):
        panel = jnp.where(slot == index, refs[index][...], panel)
    return panel


def low_kernel(tokens, start_ref, me_ref, y_ref, *refs):
    panels, out_ref = refs[:-1], refs[-1]
    fold = Q // 2
    for block in range(FINAL_BLOCKS):
        slot = block_slot(pl.program_id(0) * FINAL_BLOCKS + block, start_ref, me_ref[0], tokens)
        low = lax.dot_general(
            y_ref[block * Q : (block + 1) * Q, :],
            chosen(slot, panels),
            (((1,), (1,)), ((), ())),
            preferred_element_type=F32,
        )
        out_ref[block * fold : (block + 1) * fold, :] = jnp.concatenate([low[:fold], low[fold:]], axis=1)


def low_part(starts, me, y, panels):
    tokens, inner = y.shape
    span = FINAL_BLOCKS * Q
    rows = lambda i, s, m: (i, 0)
    whole = lambda i, s, m: (0, 0)
    return pl.pallas_call(
        functools.partial(low_kernel, tokens),
        grid_spec=pltpu.PrefetchScalarGridSpec(
            num_scalar_prefetch=2,
            grid=(tokens // span,),
            in_specs=[pl.BlockSpec((span, inner), rows)]
            + [pl.BlockSpec(panel.shape, whole) for panel in panels],
            out_specs=pl.BlockSpec((span // 2, LANES), rows),
        ),
        out_shape=jax.ShapeDtypeStruct((tokens // 2, LANES), F32),
        compiler_params=params(62),
        cost_estimate=cost(4),
        name="low_part",
    )(starts, me, y, *panels)


def held_kernel(counts, unit, *refs):
    own, pair = refs[:Y_UNITS], refs[Y_UNITS : 2 * Y_UNITS]
    parts, out_ref = list(refs[2 * Y_UNITS : -1]), refs[-1]
    for block in range(Y_UNITS):
        total = own[block][...].astype(F32) + pair[block][...].astype(F32)
        for _ in range(counts[block]):
            total = total + parts.pop(0)[...].astype(F32)
        out_ref[:, block * unit : (block + 1) * unit] = total


def held_sum(own, pair, parts, unit):
    tokens = own.shape[0]
    tile = 2 * Q
    column = lambda at: pl.BlockSpec((tile, unit), lambda i: (i, at))
    here = [[(array, at) for array, at, block in parts if block == unit_at] for unit_at in range(Y_UNITS)]
    return pl.pallas_call(
        functools.partial(held_kernel, [len(each) for each in here], unit),
        grid=(tokens // tile,),
        in_specs=[column(block) for block in range(Y_UNITS)]
        + [column(0)] * Y_UNITS
        + [column(at) for each in here for _, at in each],
        out_specs=pl.BlockSpec((tile, Y_UNITS * unit), lambda i: (i, 0)),
        out_shape=jax.ShapeDtypeStruct((tokens, Y_UNITS * unit), F32),
        compiler_params=params(),
        cost_estimate=cost(3),
        name="held_sum",
    )(*[own] * Y_UNITS, *pair, *[array for each in here for array, _ in each])


def final_kernel(tokens, first, unit, start_ref, me_ref, low_ref, held_ref, *refs):
    panels, parts, out_ref = refs[: TURN_DEV + 1], refs[TURN_DEV + 1 : -1], refs[-1]
    rank = LANES // 2
    start = first * unit
    for block in range(FINAL_BLOCKS):
        slot = block_slot(pl.program_id(0) * FINAL_BLOCKS + block, start_ref, me_ref[0], tokens)
        low = low_ref[block * Q // 2 : (block + 1) * Q // 2, :].astype(BF16)
        low = jnp.concatenate([low[:, :rank], low[:, rank:]], axis=0)
        rows = slice(block * Q, (block + 1) * Q)
        total = held_ref[rows, :] + jnp.dot(low, chosen(slot, panels), preferred_element_type=F32)
        out_ref[rows, :start] = total[:, :start].astype(BF16)
        rest = total[:, start:]
        for part in parts:
            rest = rest + part[rows, :].astype(F32)
        out_ref[rows, start:] = rest.astype(BF16)


def final_sum(starts, me, low, held, panels, parts, first, unit):
    tokens, features = held.shape
    span = FINAL_BLOCKS * Q
    rows = lambda i, s, m: (i, 0)
    whole = lambda i, s, m: (0, 0)
    return pl.pallas_call(
        functools.partial(final_kernel, tokens, first, unit),
        grid_spec=pltpu.PrefetchScalarGridSpec(
            num_scalar_prefetch=2,
            grid=(tokens // span,),
            in_specs=[pl.BlockSpec((span // 2, LANES), rows), pl.BlockSpec((span, features), rows)]
            + [pl.BlockSpec(panel.shape, whole) for panel in panels]
            + [pl.BlockSpec((span, part.shape[1]), rows) for part in parts],
            out_specs=pl.BlockSpec((span, features), rows),
        ),
        out_shape=jax.ShapeDtypeStruct((tokens, features), BF16),
        compiler_params=params(),
        cost_estimate=cost(3),
        name="final_sum",
    )(starts, me, low, held, *panels, *parts)


def shift_up(block, axis, distance):
    devices = range(lax.axis_size(axis))
    route = [(i, i + distance) for i in devices if i + distance in devices]
    return lax.ppermute(block, axis, route)


def swap(block, axis, bits):
    return lax.ppermute(block, axis, [(i, i ^ bits) for i in range(lax.axis_size(axis))])


def after(value, *earlier):
    return lax.optimization_barrier((value, *earlier))[0] if earlier else value


def neighbour_edge(edge):
    size = lax.axis_size("ctx")
    even = lax.ppermute(edge, "ctx", [(i, i ^ 1) for i in range(size)])
    odd = lax.ppermute(edge, "ctx", [(i, i + 1 if i % 2 else i - 1) for i in range(1, size - 1)])
    return even, odd


class Route:
    def __init__(self, bits, send, keep):
        self.bits, self.send, self.held, self.size = list(bits), send, [keep], keep.shape[0]
        self.got = None

    def merge(self, *earlier):
        self.held.append(after(self.got, *earlier))
        half = self.size // 2
        self.send = sum(each[each.shape[0] - self.size : each.shape[0] - half] for each in self.held)
        self.size, self.got = half, None
        return self.send

    def step(self, *earlier):
        if not self.bits:
            return
        if self.got is not None:
            self.merge(*earlier)
        self.got = swap(after(self.send, *earlier), "ctx", self.bits.pop(0))

    def end(self, *earlier):
        while self.bits:
            self.step(*earlier)
        self.held.append(after(self.got, *earlier))
        return sum(each[-1] for each in self.held)


def unpacked(packed):
    decay = packed[N : N + 1].astype(F32) + packed[N + 1 : N + 2].astype(F32)
    return packed[:N].astype(F32), decay


def packed(state, decay):
    high = decay.astype(BF16)
    low = (decay - high.astype(F32)).astype(BF16)
    fill = jnp.zeros((HALO - 2, state.shape[1]), BF16)
    return jnp.concatenate([state.astype(BF16), high, low, fill], axis=0)


def local(
    input_x_channels,
    input_b_channels,
    input_c_channels,
    input_gate_channels,
    raw_step_sizes,
    log_decay_rate,
    head_skip_coeff,
    x_conv_taps,
    b_conv_taps,
    c_conv_taps,
    gated_norm_gain,
    output_weight,
    adapter_down_panels,
    adapter_up_panels,
    turn_first_token,
    tenant_of_turn,
    tenant_panel_index,
):
    tokens, inner = input_x_channels.shape
    heads = log_decay_rate.shape[0]
    blocks = tokens // Q
    features = adapter_up_panels.shape[2]
    unit = features // Y_UNITS
    ctx = lax.axis_index("ctx").astype(jnp.int32)
    head = lax.axis_index("head").astype(jnp.int32)
    devices = lax.axis_size("ctx")
    parity = ctx % 2
    first = parity == 0
    me = ctx[None]
    parity_arg, head_arg = parity[None], head[None]
    down = jnp.swapaxes(adapter_down_panels, 1, 2)
    up = adapter_up_panels
    outer = [1 << bit for bit in range(1, devices.bit_length() - 1)]
    near, far = [1] + outer, outer + [1]

    edge = sequence_edge(input_x_channels, input_b_channels, input_c_channels)
    halos = neighbour_edge(edge)

    slots = range(TURN_DEV)

    def pack(jobs, *earlier):
        packs = pack_panels(jobs, tenant_panel_index, tenant_of_turn, after(me, *earlier), devices)
        return [Route(bits, *each) for (_, bits, _), each in zip(jobs, packs)]

    down_early, down_late, ups = pack(
        [(down, far, slots[:1]), (down, near, slots[1:]), (up, near, slots)]
    )
    packed_first = down_early.send
    down_early.step()
    down_late.step()

    lane_head = np.arange(inner) // P_SIZE
    spread = jnp.asarray(
        (np.arange(2 * heads)[:, None] % heads == lane_head[None, :]).astype(ml_dtypes.bfloat16)
    )
    xc, bc, run, shifted, before, start, keep, send = local_states(
        after(parity_arg, packed_first),
        input_x_channels,
        input_b_channels,
        halos,
        raw_step_sizes,
        log_decay_rate[None],
        x_conv_taps,
        b_conv_taps,
        spread,
    )
    count = blocks // PIECES

    def mix_piece(piece, held, *earlier):
        return mix(
            piece * count, count, after(parity_arg, *earlier), xc, bc, input_c_channels, halos, run, shifted,
            before, start, input_gate_channels, head_skip_coeff[None], c_conv_taps, spread, held,
        )

    got = swap(send, "ctx", 1)
    held = mix_piece(0, None, send)
    got = after(got, held[2])
    own_state, own_decay = unpacked(keep)
    got_state, got_decay = unpacked(got)
    first_state = jnp.where(first, own_state, got_state)
    first_decay = jnp.where(first, own_decay, got_decay)
    total = jnp.where(first, got_state, own_state)
    total_decay = jnp.where(first, got_decay, own_decay)
    total, total_decay = total + total_decay * first_state, total_decay * first_decay
    ups.step(got)
    incoming = jnp.zeros_like(total)
    incoming_decay = jnp.ones_like(total_decay)
    for bit in outer:
        sent = packed(total, total_decay)
        got = swap(sent, "ctx", bit)
        if bit == outer[0]:
            got = after(got, down_early.merge(sent), down_late.merge(sent))
        if bit == outer[-1]:
            held = mix_piece(1, held, sent)
            got = after(got, held[2])
        state, decay = unpacked(got)
        upper = (ctx & bit) != 0
        incoming = jnp.where(upper, incoming + incoming_decay * state, incoming)
        incoming_decay = jnp.where(upper, incoming_decay * decay, incoming_decay)
        total, total_decay = (
            jnp.where(upper, total + total_decay * state, state + decay * total),
            total_decay * decay,
        )
    down_early.step(held[2])
    down_late.step(held[2])
    incoming_second = first_state + first_decay * incoming
    back_sent = jnp.where(first, incoming_second, incoming).astype(BF16)
    kept = jnp.where(first, incoming, incoming_second).astype(BF16)
    back = swap(back_sent, "ctx", 1)
    part, scale, cc = held

    chips = range(1, lax.axis_size("head") // 2)
    first, later = range(Y_FIRST), range(Y_FIRST, Y_UNITS)

    def side(units, core):
        return [(2 * chip ^ core, at) for chip in chips for at in units]

    parts = []

    def send_both(mine, to_pair, units, *earlier):
        from_pair = swap(after(to_pair, *earlier), "head", 1)
        sums = []
        for chip in chips:
            columns = slice((chip - 1) * len(units) * unit, chip * len(units) * unit)
            both = (mine[:, columns].astype(F32) + from_pair[:, columns].astype(F32)).astype(BF16)
            arrived = swap(both, "head", 2 * chip)
            parts.extend((arrived, at - units.start, at) for at in units)
            sums.append(both)
        return sums

    routes = (down_late, down_early, ups)
    y_normed, to_pair, mine = norm_project(
        parity_arg, head_arg, side(first, 1) + side(first, 0), part, scale, cc, kept, back,
        gated_norm_gain[None], output_weight, unit,
    )
    sums = send_both(mine, to_pair, first, down_early.got, down_late.got, ups.got)
    down_late.step(*sums)
    down_early.step(*sums)
    ups.step(*sums)
    to_pair, mine, *own_to_pair = project_rest(
        after(head_arg, *sums),
        [side(later, 1), side(later, 0)] + [[(1, at)] for at in range(Y_UNITS)],
        y_normed, output_weight, unit, 1,
    )
    sums = send_both(
        mine, to_pair, later,
        *[arrived for arrived, _, _ in parts], down_early.got, down_late.got, ups.got,
    )
    ups.step(*sums)
    down_second = down_late.end(*sums)
    down_first = down_early.end(*sums)
    down_before = shift_up(down_second, "ctx", 1)
    pair = [swap(after(each, *sums), "head", 1) for each in own_to_pair]
    (own,) = project_rest(
        after(head_arg, down_second, down_first),
        [[(0, at) for at in range(Y_UNITS)]],
        y_normed, output_weight, unit, 1,
    )
    up_own = ups.end(own)
    rank = up.shape[1]
    up_first, up_second = up_own[:rank], up_own[rank:]
    up_before = shift_up(up_second, "ctx", 1)
    low = low_part(
        after(turn_first_token, own, ups.got), me, y_normed, [down_before, down_first, down_second]
    )
    low = low + swap(after(low, up_before), "head", 1)
    low_sent = after(low.astype(BF16), *[arrived for arrived, _, _ in parts])
    for chip in chips:
        low = low + swap(low_sent, "head", 2 * chip).astype(F32)
    here = [each for each in parts if each[2] in first]
    held = held_sum(own, pair, here, unit)
    last = [arrived for arrived, at, _ in parts[len(here) :] if at == 0]
    return final_sum(
        turn_first_token, me, low, held, [up_before, up_first, up_second], last, Y_FIRST, unit
    )


def solution(mesh):
    in_specs = (
        P("ctx", "head"),
        P("ctx", "head"),
        P("ctx", "head"),
        P("ctx", "head"),
        P("head", "ctx"),
        P("head"),
        P("head"),
        P(None, "head"),
        P(None, "head"),
        P(None, "head"),
        P("head"),
        P("head", None),
        P("ctx", "head", None),
        P("ctx", None, "head"),
        P(),
        P(),
        P(),
    )
    out_specs = P("ctx", "head")
    return jax.shard_map(local, mesh=mesh, in_specs=in_specs, out_specs=out_specs, check_vma=False)
```

```python
import functools

import jax
import jax.numpy as jnp
import ml_dtypes
import numpy as np
from jax import lax
from jax.experimental import pallas as pl
from jax.experimental.pallas import tpu as pltpu
from jax.sharding import PartitionSpec as P

P_SIZE = 64
N = 128
K = 4
Q = 128
TURN_DEV = 2
HALO = 16
LANES = 128
PIECES = 2
STATE_BLOCKS = 2
FINAL_BLOCKS = 2
Y_UNITS = 4
Y_FIRST = 2

F32 = jnp.float32
BF16 = jnp.bfloat16
epsilon = 1e-05
MIB = 1024 * 1024


def params(mib=28):
    return pltpu.CompilerParams(vmem_limit_bytes=mib * MIB)


def cost(microseconds):
    return pl.CostEstimate(flops=int(microseconds * 1e5), bytes_accessed=1, transcendentals=0)


def silu(v):
    half = 0.5 * v
    return half + half * jnp.tanh(half)


def conv_rows(current, previous, taps):
    rows = current.shape[0]
    joined = jnp.concatenate([previous, current], axis=0)
    total = taps[K - 1 : K] * current
    for back in range(1, K):
        total = total + taps[K - 1 - back : K - back] * pltpu.roll(joined, back, 0)[8 : 8 + rows]
    return silu(total).astype(BF16)


def two_terms(v):
    high = v.astype(BF16).astype(F32)
    return high, v - high


def column_of(row):
    size = row.shape[1]
    here = lax.broadcasted_iota(jnp.int32, (size, size), 0)
    there = lax.broadcasted_iota(jnp.int32, (size, size), 1)
    return jnp.sum(jnp.where(here == there, row, 0.0), axis=1, keepdims=True)


def pad_rows(stack):
    rows = stack.shape[0]
    if rows % LANES:
        fill = jnp.zeros((LANES - rows % LANES, stack.shape[1]), F32)
        stack = jnp.concatenate([stack, fill], axis=0)
    return stack


def edge_kernel(x_ref, b_ref, c_ref, out_ref):
    place = 0
    for ref in (x_ref, b_ref, c_ref):
        out_ref[:, place : place + ref.shape[1]] = ref[...]
        place += ref.shape[1]


def sequence_edge(*arrays):
    tokens = arrays[0].shape[0]
    width = sum(array.shape[1] for array in arrays)
    return pl.pallas_call(
        edge_kernel,
        grid=(1,),
        in_specs=[
            pl.BlockSpec((HALO, array.shape[1]), lambda i: (tokens // HALO - 1, 0)) for array in arrays
        ],
        out_specs=pl.BlockSpec((HALO, width), lambda i: (0, 0)),
        out_shape=jax.ShapeDtypeStruct((HALO, width), BF16),
        compiler_params=params(62),
        cost_estimate=cost(1),
        name="sequence_edge",
    )(*arrays)


def panel_home(place, panel_index, tenants, me, *, bits, slot, count):
    relative = 0
    for order, bit in enumerate(bits):
        relative += bit * (1 - (place >> (len(bits) - 1 - order)) % 2)
    panel = panel_index[tenants[TURN_DEV * (relative ^ me) + slot]]
    owned = lax.div(panel, count) == me
    return jnp.where(owned, lax.rem(panel, count), 0), owned


def panel_kernel(homes, devices, index_ref, tenant_ref, me_ref, *refs):
    ins, outs = refs[: len(homes)], refs[len(homes) : 3 * len(homes)]
    zeros, sems = refs[-2:]
    zeros[...] = jnp.zeros_like(zeros)
    half = devices // 2
    started = []
    for number, job in enumerate(homes):
        in_ref = ins[number]
        rows, width = in_ref.shape[1:]
        for place in range(devices):
            out_ref = outs[2 * number + (place >= half)]
            for slot, home in enumerate(job):
                local, owned = home(place, index_ref, tenant_ref, me_ref[0])
                out = out_ref.at[place % half, pl.ds(slot * rows, rows), :]
                sem = sems.at[len(started)]
                own = pltpu.make_async_copy(in_ref.at[local], out, sem)
                none = pltpu.make_async_copy(zeros.at[pl.ds(0, rows), pl.ds(0, width)], out, sem)

                @pl.when(owned)
                def _(own=own):
                    own.start()

                @pl.when(jnp.logical_not(owned))
                def _(none=none):
                    none.start()

                started.append(none)
    for copy in started:
        copy.wait()


def pack_panels(jobs, panel_index, tenants, me, devices):
    half = devices // 2
    homes, out_shape, copies = [], [], 0
    for panels, bits, slots in jobs:
        count, rows, width = panels.shape
        homes.append(
            [
                functools.partial(panel_home, bits=bits, slot=slot, count=count)
                for slot in slots
            ]
        )
        out_shape += [jax.ShapeDtypeStruct((half, len(slots) * rows, width), BF16)] * 2
        copies += devices * len(slots)
    zero_shape = tuple(max(panels.shape[axis] for panels, _, _ in jobs) for axis in (1, 2))
    outs = pl.pallas_call(
        functools.partial(panel_kernel, homes, devices),
        grid_spec=pltpu.PrefetchScalarGridSpec(
            num_scalar_prefetch=3,
            grid=(1,),
            in_specs=[pl.BlockSpec(job[0].shape, lambda i, *_: (0, 0, 0)) for job in jobs],
            out_specs=[pl.BlockSpec(memory_space=pl.ANY)] * len(out_shape),
            scratch_shapes=[pltpu.VMEM(zero_shape, BF16), pltpu.SemaphoreType.DMA((copies,))],
        ),
        out_shape=out_shape,
        compiler_params=params(50),
        cost_estimate=cost(5),
        name="pack_panels",
    )(panel_index, tenants, me, *[job[0] for job in jobs])
    return [outs[2 * job : 2 * job + 2] for job in range(len(jobs))]


def state_kernel(
    parity_ref, x_ref, b_ref, even_ref, odd_ref, raw_ref, rate_ref, xt_ref, bt_ref, spread_ref,
    xc_ref, bc_ref, run_ref, shifted_ref, before_ref, start_ref, keep_ref, send_ref,
    x_prev, b_prev, weight, x_weighted, state, decay_product,
):
    block = pl.program_id(0)
    inner = x_ref.shape[1]
    bc_width = b_ref.shape[1]
    groups = bc_width // N
    width = inner // groups

    @pl.when(block == 0)
    def _():
        halo = jnp.where(parity_ref[0] == 1, even_ref[...], odd_ref[...])
        x_prev[...] = halo[:, :inner].astype(F32)[8:]
        b_prev[...] = halo[:, inner : inner + bc_width].astype(F32)[8:]
        state[...] = jnp.zeros_like(state)
        decay_product[...] = jnp.ones_like(decay_product)

    raw = raw_ref[...]
    step = jnp.maximum(raw, 0.0) + jnp.log1p(jnp.exp(-jnp.abs(raw)))
    change = -step * jnp.exp(column_of(rate_ref[...]))
    heads = raw.shape[0]
    first = change.astype(BF16)
    rest = change - first.astype(F32)
    second = rest.astype(BF16)
    third = (rest - second.astype(F32)).astype(BF16)
    terms = jnp.concatenate([first, second, third], axis=0)
    upper = (
        lax.broadcasted_iota(jnp.int32, (Q, Q), 0) <= lax.broadcasted_iota(jnp.int32, (Q, Q), 1)
    ).astype(F32).astype(BF16)
    spread = spread_ref[...]
    parts = [slice(part * Q, (part + 1) * Q) for part in range(STATE_BLOCKS)]
    decay_rows = []
    for rows in parts:
        sums = jnp.dot(terms[:, rows], upper, preferred_element_type=F32)
        run = sums[:heads] + sums[heads : 2 * heads] + sums[2 * heads :]
        run_ref[:, rows] = run
        shifted_ref[:, rows] = jnp.log(step[:, rows]) - run
        last = run[:, Q - 1 : Q]
        tail = jnp.exp(last - run) * step[:, rows]
        whole = jnp.broadcast_to(jnp.exp(last), (heads, Q))
        columns = pad_rows(jnp.concatenate([*two_terms(tail), *two_terms(whole)], axis=0)).T
        weight[rows, :] = jnp.dot(
            columns[:, : 2 * heads].astype(BF16), spread, preferred_element_type=F32
        )
        decay_rows.append(
            jnp.dot(columns[:16, 2 * heads : 4 * heads].astype(BF16), spread, preferred_element_type=F32)[:8]
        )

    bc = conv_rows(b_ref[...].astype(F32), b_prev[...], bt_ref[...].astype(F32))
    b_prev[...] = b_ref[STATE_BLOCKS * Q - HALO :, :].astype(F32)[8:]
    bc_ref[...] = bc

    def conv_lanes(part, carried):
        lanes = pl.ds(pl.multiple_of(part * LANES, LANES), LANES)
        current = x_ref[:, lanes].astype(F32)
        xc = conv_rows(current, x_prev[:, lanes], xt_ref[:, lanes].astype(F32))
        x_prev[:, lanes] = current[STATE_BLOCKS * Q - 8 :]
        xc_ref[:, lanes] = xc
        x_weighted[:, lanes] = (xc.astype(F32) * weight[:, lanes]).astype(BF16)
        return carried

    lax.fori_loop(0, inner // LANES, conv_lanes, 0, unroll=16)

    for part, (rows, decay_row) in enumerate(zip(parts, decay_rows)):
        start_ref[part * 8 : (part + 1) * 8, :] = decay_product[...]
        decay_product[...] = decay_product[...] * decay_row
        for group in range(groups):
            lanes = slice(group * width, (group + 1) * width)
            fresh = lax.dot_general(
                bc[rows, group * N : (group + 1) * N],
                x_weighted[rows, lanes],
                (((0,), (0,)), ((), ())),
                preferred_element_type=F32,
            )
            held = state[:, lanes]
            before_ref[part * N : (part + 1) * N, lanes] = held.astype(BF16)
            state[:, lanes] = held * decay_row[:1, lanes] + fresh

    @pl.when(block == pl.num_programs(0) - 1)
    def _():
        half = inner // 2
        row = lax.broadcasted_iota(jnp.int32, (HALO, half), 0)
        for out_ref, place in ((keep_ref, parity_ref[0]), (send_ref, 1 - parity_ref[0])):
            lanes = pl.ds(pl.multiple_of(place * half, LANES), half)
            out_ref[:N] = state[:, lanes].astype(BF16)
            high, low = two_terms(decay_product[:1, lanes])
            out_ref[N:] = jnp.where(row == 0, high, jnp.where(row == 1, low, 0.0)).astype(BF16)


def local_states(parity, x, b, halos, raw, rate, x_taps, b_taps, spread):
    tokens, inner = x.shape
    bc_width = b.shape[1]
    heads = raw.shape[0]
    blocks = tokens // Q
    half = inner // 2
    span = STATE_BLOCKS * Q
    whole = lambda c, p: (0, 0)
    rows = lambda c, p: (c, 0)
    columns = lambda c, p: (0, c)
    return pl.pallas_call(
        state_kernel,
        grid_spec=pltpu.PrefetchScalarGridSpec(
            num_scalar_prefetch=1,
            grid=(blocks // STATE_BLOCKS,),
            in_specs=[
                pl.BlockSpec((span, inner), rows),
                pl.BlockSpec((span, bc_width), rows),
                pl.BlockSpec(halos[0].shape, whole),
                pl.BlockSpec(halos[0].shape, whole),
                pl.BlockSpec((heads, span), columns),
                pl.BlockSpec((1, heads), whole),
                pl.BlockSpec((K, inner), whole),
                pl.BlockSpec((K, bc_width), whole),
                pl.BlockSpec(spread.shape, whole),
            ],
            out_specs=[
                pl.BlockSpec((span, inner), rows),
                pl.BlockSpec((span, bc_width), rows),
                pl.BlockSpec((heads, span), columns),
                pl.BlockSpec((heads, span), columns),
                pl.BlockSpec((STATE_BLOCKS * N, inner), rows),
                pl.BlockSpec((STATE_BLOCKS * 8, inner), rows),
                pl.BlockSpec((N + HALO, half), whole),
                pl.BlockSpec((N + HALO, half), whole),
            ],
            scratch_shapes=[
                pltpu.VMEM((8, inner), F32),
                pltpu.VMEM((8, bc_width), F32),
                pltpu.VMEM((span, inner), F32),
                pltpu.VMEM((span, inner), BF16),
                pltpu.VMEM((N, inner), F32),
                pltpu.VMEM((8, inner), F32),
            ],
        ),
        out_shape=[
            jax.ShapeDtypeStruct((tokens, inner), BF16),
            jax.ShapeDtypeStruct((tokens, bc_width), BF16),
            jax.ShapeDtypeStruct((heads, tokens), F32),
            jax.ShapeDtypeStruct((heads, tokens), F32),
            jax.ShapeDtypeStruct((blocks * N, inner), BF16),
            jax.ShapeDtypeStruct((blocks * 8, inner), F32),
            jax.ShapeDtypeStruct((N + HALO, half), BF16),
            jax.ShapeDtypeStruct((N + HALO, half), BF16),
        ],
        compiler_params=params(50),
        cost_estimate=cost(150000),
        name="local_states",
    )(parity, x, b, *halos, raw, rate, x_taps, b_taps, spread)


def mix_kernel(
    first, has_alias, parity_ref, *refs
):
    (
        xc_ref, bc_ref, c_ref, c_prev_ref, even_ref, odd_ref, run_ref, shifted_ref, before_ref, start_ref,
        gate_ref, skip_ref, ct_ref, spread_ref,
    ) = refs[:14]
    refs = refs[14 + (3 if has_alias else 0) :]
    part_ref, scale_ref, cc_ref, rise = refs
    block = pl.program_id(0) + first
    inner = xc_ref.shape[1]
    bc_width = c_ref.shape[1]
    groups = bc_width // N
    width = inner // groups
    heads = run_ref.shape[0]

    at = slice(inner + bc_width, inner + 2 * bc_width)
    c_halo = jnp.where(parity_ref[0] == 1, even_ref[:, at], odd_ref[:, at]).astype(F32)[8:]
    c_before = jnp.where(block == 0, c_halo, c_prev_ref[...].astype(F32)[8:])
    cc = conv_rows(c_ref[...].astype(F32), c_before, ct_ref[...].astype(F32))
    cc_ref[...] = cc
    run = run_ref[...]
    columns = pad_rows(jnp.concatenate([*two_terms(jnp.exp(run)), run], axis=0)).T
    rise[...] = jnp.dot(
        columns[:, : 2 * heads].astype(BF16), spread_ref[...], preferred_element_type=F32
    )
    skips = jnp.broadcast_to(jnp.concatenate(two_terms(skip_ref[...]), axis=1), (16, 2 * heads))
    skip = jnp.dot(skips.astype(BF16), spread_ref[...], preferred_element_type=F32)[:1]
    causal = lax.broadcasted_iota(jnp.int32, (Q, Q), 0) >= lax.broadcasted_iota(jnp.int32, (Q, Q), 1)
    left = lax.broadcasted_iota(jnp.int32, (Q, LANES), 1) < P_SIZE
    for group in range(groups):
        state_lanes = slice(group * N, (group + 1) * N)
        scores = lax.dot_general(
            cc[:, state_lanes],
            bc_ref[:, state_lanes],
            (((1,), (1,)), ((), ())),
            preferred_element_type=F32,
        )
        scores = jnp.where(causal, scores, 0.0)
        for pair in range(width // LANES):
            lanes = slice(group * width + pair * LANES, group * width + (pair + 1) * LANES)
            mixing = []
            for head in (lanes.start // P_SIZE, lanes.start // P_SIZE + 1):
                gap = columns[:, 2 * heads + head : 2 * heads + head + 1] + shifted_ref[head : head + 1, :]
                mixing.append((scores * jnp.exp(jnp.where(causal, gap, 0.0))).astype(BF16))
            x = xc_ref[:, lanes].astype(F32)
            x_pair = jnp.concatenate(
                [jnp.where(left, x, 0.0).astype(BF16), jnp.where(left, 0.0, x).astype(BF16)], axis=0
            )
            y = jnp.dot(jnp.concatenate(mixing, axis=1), x_pair, preferred_element_type=F32)
            carried = jnp.dot(cc[:, state_lanes], before_ref[:, lanes], preferred_element_type=F32)
            rise_part = rise[:, lanes]
            y = y + rise_part * carried + skip[:, lanes] * x
            gate = silu(gate_ref[:, lanes].astype(F32))
            part_ref[:, lanes] = (y * gate).astype(BF16)
            scale_ref[:, lanes] = (gate * rise_part * start_ref[:1, lanes]).astype(BF16)


def mix(
    first, count, parity, xc, bc, c, halos, run, shifted, before, start, gate, skip, c_taps, spread, held
):
    tokens, inner = xc.shape
    bc_width = c.shape[1]
    heads = run.shape[0]
    whole = lambda i, p: (0, 0)
    rows = lambda i, p: (first + i, 0)
    columns = lambda i, p: (0, first + i)
    per_block = Q // HALO
    any_spec = pl.BlockSpec(memory_space=pl.ANY)
    aliased = list(held) if held is not None else []
    return pl.pallas_call(
        functools.partial(mix_kernel, first, bool(aliased)),
        grid_spec=pltpu.PrefetchScalarGridSpec(
            num_scalar_prefetch=1,
            grid=(count,),
            in_specs=[
                pl.BlockSpec((Q, inner), rows),
                pl.BlockSpec((Q, bc_width), rows),
                pl.BlockSpec((Q, bc_width), rows),
                pl.BlockSpec(
                    (HALO, bc_width), lambda i, p: (jnp.maximum((first + i) * per_block - 1, 0), 0)
                ),
                pl.BlockSpec(halos[0].shape, whole),
                pl.BlockSpec(halos[0].shape, whole),
                pl.BlockSpec((heads, Q), columns),
                pl.BlockSpec((heads, Q), columns),
                pl.BlockSpec((N, inner), rows),
                pl.BlockSpec((8, inner), rows),
                pl.BlockSpec((Q, inner), rows),
                pl.BlockSpec((1, heads), whole),
                pl.BlockSpec((K, bc_width), whole),
                pl.BlockSpec(spread.shape, whole),
            ]
            + [any_spec] * len(aliased),
            out_specs=[
                pl.BlockSpec((Q, inner), rows),
                pl.BlockSpec((Q, inner), rows),
                pl.BlockSpec((Q, bc_width), rows),
            ],
            scratch_shapes=[pltpu.VMEM((Q, inner), F32)],
        ),
        out_shape=[
            jax.ShapeDtypeStruct((tokens, inner), BF16),
            jax.ShapeDtypeStruct((tokens, inner), BF16),
            jax.ShapeDtypeStruct((tokens, bc_width), BF16),
        ],
        input_output_aliases={15 + i: i for i in range(len(aliased))},
        compiler_params=params(50),
        cost_estimate=cost(count * 25000),
        name="mix",
    )(parity, xc, bc, c, c, *halos, run, shifted, before, start, gate, skip, c_taps, spread, *aliased)


def project_unit(y_ref, w_ref, send_ref, keep_ref, step, units):
    @pl.when(step < units)
    def _():
        send_ref[...] = jnp.dot(y_ref[...], w_ref[...], preferred_element_type=F32).astype(BF16)

    @pl.when(step >= units)
    def _():
        keep_ref[...] = jnp.dot(y_ref[...], w_ref[...], preferred_element_type=F32).astype(BF16)


def norm_kernel(
    tiles, parity_ref, place_ref, part_ref, scale_ref, cc_ref, keep_state_ref, got_ref, gain_ref, w_ref,
    out_ref, send_ref, keep_ref, state,
):
    inner = part_ref.shape[1]
    groups = cc_ref.shape[1] // N
    width = inner // groups
    half = inner // 2
    step = pl.program_id(0)
    tile = part_ref.shape[0]

    @pl.when(step == 0)
    def _():
        for ref, place in ((keep_state_ref, parity_ref[0]), (got_ref, 1 - parity_ref[0])):
            state[:, pl.ds(pl.multiple_of(place * half, LANES), half)] = ref[...]

    @pl.when(step < tiles)
    def _():
        rows = pl.ds(pl.multiple_of(step * tile, tile), tile)
        for group in range(groups):
            lanes = slice(group * width, (group + 1) * width)
            carried = jnp.dot(
                cc_ref[:, group * N : (group + 1) * N], state[:, lanes], preferred_element_type=F32
            )
            gated = part_ref[:, lanes].astype(F32) + scale_ref[:, lanes].astype(F32) * carried
            mean = jnp.sum(gated * gated, axis=1, keepdims=True) * (1.0 / width)
            normed = gated * lax.rsqrt(mean + epsilon) * gain_ref[:, lanes].astype(F32)
            out_ref[rows, lanes] = normed.astype(BF16)

    @pl.when(step >= tiles)
    def _():
        project_unit(out_ref, w_ref, send_ref, keep_ref, step - tiles, pl.num_programs(0) // 2 - tiles // 2)


def norm_project(parity, head, blocks, part, scale, cc, keep, got, gain, weight, width):
    tokens, inner = part.shape
    tile = 2 * Q
    tiles = tokens // tile
    units = len(blocks) // 2
    place = place_of(blocks)
    whole = lambda i, p, q: (0, 0)
    rows = lambda i, p, q: (jnp.minimum(i, tiles - 1), 0)
    return pl.pallas_call(
        functools.partial(norm_kernel, tiles),
        grid_spec=pltpu.PrefetchScalarGridSpec(
            num_scalar_prefetch=2,
            grid=(tiles + 2 * units,),
            in_specs=[
                pl.BlockSpec((tile, inner), rows),
                pl.BlockSpec((tile, inner), rows),
                pl.BlockSpec((tile, cc.shape[1]), rows),
                pl.BlockSpec(keep.shape, whole),
                pl.BlockSpec(got.shape, whole),
                pl.BlockSpec((1, inner), whole),
                pl.BlockSpec((inner, width), lambda i, p, q: (0, place(jnp.maximum(i - tiles, 0), q[0]))),
            ],
            out_specs=[
                pl.BlockSpec((tokens, inner), whole),
                pl.BlockSpec((tokens, width), lambda i, p, q: (0, jnp.clip(i - tiles, 0, units - 1))),
                pl.BlockSpec((tokens, width), lambda i, p, q: (0, jnp.maximum(i - tiles - units, 0))),
            ],
            scratch_shapes=[pltpu.VMEM((N, inner), BF16)],
        ),
        out_shape=[
            jax.ShapeDtypeStruct((tokens, inner), BF16),
            jax.ShapeDtypeStruct((tokens, units * width), BF16),
            jax.ShapeDtypeStruct((tokens, units * width), BF16),
        ],
        compiler_params=params(50),
        cost_estimate=cost(11),
        name="norm_project",
    )(parity, head, part, scale, cc, keep, got, gain, weight)


def place_of(blocks):
    def column(step, head):
        column = (head ^ blocks[0][0]) * Y_UNITS + blocks[0][1]
        for index, (bits, unit) in enumerate(blocks[1:], 1):
            column = jnp.where(step == index, (head ^ bits) * Y_UNITS + unit, column)
        return column

    return column


def rest_kernel(counts, head_ref, y_ref, w_ref, *outs):
    step = pl.program_id(0)
    start = 0
    for count, out_ref in zip(counts, outs):

        @pl.when((step >= start) & (step < start + count))
        def _(out_ref=out_ref):
            out_ref[...] = jnp.dot(y_ref[...], w_ref[...], preferred_element_type=F32).astype(BF16)

        start += count


def project_rest(head, sides, y, weight, width, microseconds):
    tokens, inner = y.shape
    counts = [len(side) for side in sides]
    blocks = [block for side in sides for block in side]
    place = place_of(blocks)
    out_specs, start = [], 0
    for count in counts:
        out_specs.append(
            pl.BlockSpec(
                (tokens, width),
                lambda i, p, start=start, count=count: (0, jnp.clip(i - start, 0, count - 1)),
            )
        )
        start += count
    return pl.pallas_call(
        functools.partial(rest_kernel, counts),
        grid_spec=pltpu.PrefetchScalarGridSpec(
            num_scalar_prefetch=1,
            grid=(len(blocks),),
            in_specs=[
                pl.BlockSpec((tokens, inner), lambda i, p: (0, 0)),
                pl.BlockSpec((inner, width), lambda i, p: (0, place(i, p[0]))),
            ],
            out_specs=out_specs,
        ),
        out_shape=[jax.ShapeDtypeStruct((tokens, count * width), BF16) for count in counts],
        compiler_params=params(46),
        cost_estimate=cost(microseconds),
        name="project_rest",
    )(head, y, weight)


def block_slot(block, starts, me, tokens):
    place = me * tokens + block * Q
    slot = 0
    for turn in range(TURN_DEV):
        slot = slot + (starts[TURN_DEV * me + turn] <= place).astype(jnp.int32)
    return slot


def chosen(slot, refs):
    panel = refs[0][...]
    for index in range(1, len(refs)):
        panel = jnp.where(slot == index, refs[index][...], panel)
    return panel


def low_kernel(tokens, start_ref, me_ref, y_ref, *refs):
    panels, out_ref = refs[:-1], refs[-1]
    fold = Q // 2
    for block in range(FINAL_BLOCKS):
        slot = block_slot(pl.program_id(0) * FINAL_BLOCKS + block, start_ref, me_ref[0], tokens)
        low = lax.dot_general(
            y_ref[block * Q : (block + 1) * Q, :],
            chosen(slot, panels),
            (((1,), (1,)), ((), ())),
            preferred_element_type=F32,
        )
        out_ref[block * fold : (block + 1) * fold, :] = jnp.concatenate([low[:fold], low[fold:]], axis=1)


def low_part(starts, me, y, panels):
    tokens, inner = y.shape
    span = FINAL_BLOCKS * Q
    rows = lambda i, s, m: (i, 0)
    whole = lambda i, s, m: (0, 0)
    return pl.pallas_call(
        functools.partial(low_kernel, tokens),
        grid_spec=pltpu.PrefetchScalarGridSpec(
            num_scalar_prefetch=2,
            grid=(tokens // span,),
            in_specs=[pl.BlockSpec((span, inner), rows)]
            + [pl.BlockSpec(panel.shape, whole) for panel in panels],
            out_specs=pl.BlockSpec((span // 2, LANES), rows),
        ),
        out_shape=jax.ShapeDtypeStruct((tokens // 2, LANES), F32),
        compiler_params=params(46),
        cost_estimate=cost(4),
        name="low_part",
    )(starts, me, y, *panels)


def held_kernel(counts, unit, *refs):
    own, pair = refs[:Y_UNITS], refs[Y_UNITS : 2 * Y_UNITS]
    parts, out_ref = list(refs[2 * Y_UNITS : -1]), refs[-1]
    for block in range(Y_UNITS):
        total = own[block][...].astype(F32) + pair[block][...].astype(F32)
        for _ in range(counts[block]):
            total = total + parts.pop(0)[...].astype(F32)
        out_ref[:, block * unit : (block + 1) * unit] = total


def held_sum(own, pair, parts, unit):
    tokens = own.shape[0]
    tile = 2 * Q
    column = lambda at: pl.BlockSpec((tile, unit), lambda i: (i, at))
    here = [[(array, at) for array, at, block in parts if block == unit_at] for unit_at in range(Y_UNITS)]
    return pl.pallas_call(
        functools.partial(held_kernel, [len(each) for each in here], unit),
        grid=(tokens // tile,),
        in_specs=[column(block) for block in range(Y_UNITS)]
        + [column(0)] * Y_UNITS
        + [column(at) for each in here for _, at in each],
        out_specs=pl.BlockSpec((tile, Y_UNITS * unit), lambda i: (i, 0)),
        out_shape=jax.ShapeDtypeStruct((tokens, Y_UNITS * unit), F32),
        compiler_params=params(),
        cost_estimate=cost(3),
        name="held_sum",
    )(*[own] * Y_UNITS, *pair, *[array for each in here for array, _ in each])


def final_kernel(tokens, first, unit, start_ref, me_ref, low_ref, held_ref, *refs):
    panels, parts, out_ref = refs[: TURN_DEV + 1], refs[TURN_DEV + 1 : -1], refs[-1]
    rank = LANES // 2
    start = first * unit
    for block in range(FINAL_BLOCKS):
        slot = block_slot(pl.program_id(0) * FINAL_BLOCKS + block, start_ref, me_ref[0], tokens)
        low = low_ref[block * Q // 2 : (block + 1) * Q // 2, :].astype(BF16)
        low = jnp.concatenate([low[:, :rank], low[:, rank:]], axis=0)
        rows = slice(block * Q, (block + 1) * Q)
        total = held_ref[rows, :] + jnp.dot(low, chosen(slot, panels), preferred_element_type=F32)
        out_ref[rows, :start] = total[:, :start].astype(BF16)
        rest = total[:, start:]
        for part in parts:
            rest = rest + part[rows, :].astype(F32)
        out_ref[rows, start:] = rest.astype(BF16)


def final_sum(starts, me, low, held, panels, parts, first, unit):
    tokens, features = held.shape
    span = FINAL_BLOCKS * Q
    rows = lambda i, s, m: (i, 0)
    whole = lambda i, s, m: (0, 0)
    return pl.pallas_call(
        functools.partial(final_kernel, tokens, first, unit),
        grid_spec=pltpu.PrefetchScalarGridSpec(
            num_scalar_prefetch=2,
            grid=(tokens // span,),
            in_specs=[pl.BlockSpec((span // 2, LANES), rows), pl.BlockSpec((span, features), rows)]
            + [pl.BlockSpec(panel.shape, whole) for panel in panels]
            + [pl.BlockSpec((span, part.shape[1]), rows) for part in parts],
            out_specs=pl.BlockSpec((span, features), rows),
        ),
        out_shape=jax.ShapeDtypeStruct((tokens, features), BF16),
        compiler_params=params(),
        cost_estimate=cost(3),
        name="final_sum",
    )(starts, me, low, held, *panels, *parts)


def shift_up(block, axis, distance):
    devices = range(lax.axis_size(axis))
    route = [(i, i + distance) for i in devices if i + distance in devices]
    return lax.ppermute(block, axis, route)


def swap(block, axis, bits):
    return lax.ppermute(block, axis, [(i, i ^ bits) for i in range(lax.axis_size(axis))])


def after(value, *earlier):
    return lax.optimization_barrier((value, *earlier))[0] if earlier else value


def neighbour_edge(edge):
    size = lax.axis_size("ctx")
    even = lax.ppermute(edge, "ctx", [(i, i ^ 1) for i in range(size)])
    odd = lax.ppermute(edge, "ctx", [(i, i + 1 if i % 2 else i - 1) for i in range(1, size - 1)])
    return even, odd


class Route:
    def __init__(self, bits, send, keep):
        self.bits, self.send, self.held, self.size = list(bits), send, [keep], keep.shape[0]
        self.got = None

    def merge(self, *earlier):
        self.held.append(after(self.got, *earlier))
        half = self.size // 2
        self.send = sum(each[each.shape[0] - self.size : each.shape[0] - half] for each in self.held)
        self.size, self.got = half, None
        return self.send

    def step(self, *earlier):
        if not self.bits:
            return
        if self.got is not None:
            self.merge(*earlier)
        self.got = swap(after(self.send, *earlier), "ctx", self.bits.pop(0))

    def end(self, *earlier):
        while self.bits:
            self.step(*earlier)
        self.held.append(after(self.got, *earlier))
        return sum(each[-1] for each in self.held)


def unpacked(packed):
    decay = packed[N : N + 1].astype(F32) + packed[N + 1 : N + 2].astype(F32)
    return packed[:N].astype(F32), decay


def packed(state, decay):
    high = decay.astype(BF16)
    low = (decay - high.astype(F32)).astype(BF16)
    fill = jnp.zeros((HALO - 2, state.shape[1]), BF16)
    return jnp.concatenate([state.astype(BF16), high, low, fill], axis=0)


def local(
    input_x_channels,
    input_b_channels,
    input_c_channels,
    input_gate_channels,
    raw_step_sizes,
    log_decay_rate,
    head_skip_coeff,
    x_conv_taps,
    b_conv_taps,
    c_conv_taps,
    gated_norm_gain,
    output_weight,
    adapter_down_panels,
    adapter_up_panels,
    turn_first_token,
    tenant_of_turn,
    tenant_panel_index,
):
    tokens, inner = input_x_channels.shape
    heads = log_decay_rate.shape[0]
    blocks = tokens // Q
    features = adapter_up_panels.shape[2]
    unit = features // Y_UNITS
    ctx = lax.axis_index("ctx").astype(jnp.int32)
    head = lax.axis_index("head").astype(jnp.int32)
    devices = lax.axis_size("ctx")
    parity = ctx % 2
    first = parity == 0
    me = ctx[None]
    parity_arg, head_arg = parity[None], head[None]
    down = jnp.swapaxes(adapter_down_panels, 1, 2)
    up = adapter_up_panels
    outer = [1 << bit for bit in range(1, devices.bit_length() - 1)]
    near, far = [1] + outer, outer + [1]

    edge = sequence_edge(input_x_channels, input_b_channels, input_c_channels)
    halos = neighbour_edge(edge)

    slots = range(TURN_DEV)

    def pack(jobs, *earlier):
        packs = pack_panels(jobs, tenant_panel_index, tenant_of_turn, after(me, *earlier), devices)
        return [Route(bits, *each) for (_, bits, _), each in zip(jobs, packs)]

    down_early, down_late, ups = pack(
        [(down, far, slots[:1]), (down, near, slots[1:]), (up, near, slots)]
    )
    packed_first = down_early.send
    down_early.step()
    down_late.step()

    lane_head = np.arange(inner) // P_SIZE
    spread = jnp.asarray(
        (np.arange(2 * heads)[:, None] % heads == lane_head[None, :]).astype(ml_dtypes.bfloat16)
    )
    xc, bc, run, shifted, before, start, keep, send = local_states(
        after(parity_arg, packed_first),
        input_x_channels,
        input_b_channels,
        halos,
        raw_step_sizes,
        log_decay_rate[None],
        x_conv_taps,
        b_conv_taps,
        spread,
    )
    count = blocks // PIECES

    def mix_piece(piece, held, *earlier):
        return mix(
            piece * count, count, after(parity_arg, *earlier), xc, bc, input_c_channels, halos, run, shifted,
            before, start, input_gate_channels, head_skip_coeff[None], c_conv_taps, spread, held,
        )

    got = swap(send, "ctx", 1)
    held = mix_piece(0, None, send)
    got = after(got, held[2])
    own_state, own_decay = unpacked(keep)
    got_state, got_decay = unpacked(got)
    first_state = jnp.where(first, own_state, got_state)
    first_decay = jnp.where(first, own_decay, got_decay)
    total = jnp.where(first, got_state, own_state)
    total_decay = jnp.where(first, got_decay, own_decay)
    total, total_decay = total + total_decay * first_state, total_decay * first_decay
    ups.step(got)
    incoming = jnp.zeros_like(total)
    incoming_decay = jnp.ones_like(total_decay)
    for bit in outer:
        sent = packed(total, total_decay)
        got = swap(sent, "ctx", bit)
        if bit == outer[0]:
            got = after(got, down_early.merge(sent), down_late.merge(sent))
        if bit == outer[-1]:
            held = mix_piece(1, held, sent)
            got = after(got, held[2])
        state, decay = unpacked(got)
        upper = (ctx & bit) != 0
        incoming = jnp.where(upper, incoming + incoming_decay * state, incoming)
        incoming_decay = jnp.where(upper, incoming_decay * decay, incoming_decay)
        total, total_decay = (
            jnp.where(upper, total + total_decay * state, state + decay * total),
            total_decay * decay,
        )
    down_early.step(held[2])
    down_late.step(held[2])
    incoming_second = first_state + first_decay * incoming
    back_sent = jnp.where(first, incoming_second, incoming).astype(BF16)
    kept = jnp.where(first, incoming, incoming_second).astype(BF16)
    back = swap(back_sent, "ctx", 1)
    part, scale, cc = held

    chips = range(1, lax.axis_size("head") // 2)
    first, later = range(Y_FIRST), range(Y_FIRST, Y_UNITS)

    def side(units, core):
        return [(2 * chip ^ core, at) for chip in chips for at in units]

    parts = []

    def send_both(mine, to_pair, units, *earlier):
        from_pair = swap(after(to_pair, *earlier), "head", 1)
        sums = []
        for chip in chips:
            columns = slice((chip - 1) * len(units) * unit, chip * len(units) * unit)
            both = (mine[:, columns].astype(F32) + from_pair[:, columns].astype(F32)).astype(BF16)
            arrived = swap(both, "head", 2 * chip)
            parts.extend((arrived, at - units.start, at) for at in units)
            sums.append(both)
        return sums

    routes = (down_late, down_early, ups)
    y_normed, to_pair, mine = norm_project(
        parity_arg, head_arg, side(first, 1) + side(first, 0), part, scale, cc, kept, back,
        gated_norm_gain[None], output_weight, unit,
    )
    sums = send_both(mine, to_pair, first, down_early.got, down_late.got, ups.got)
    down_late.step(*sums)
    down_early.step(*sums)
    ups.step(*sums)
    to_pair, mine, *own_to_pair = project_rest(
        after(head_arg, *sums),
        [side(later, 1), side(later, 0)] + [[(1, at)] for at in range(Y_UNITS)],
        y_normed, output_weight, unit, 1,
    )
    sums = send_both(
        mine, to_pair, later,
        *[arrived for arrived, _, _ in parts], down_early.got, down_late.got, ups.got,
    )
    ups.step(*sums)
    down_second = down_late.end(*sums)
    down_first = down_early.end(*sums)
    down_before = shift_up(down_second, "ctx", 1)
    pair = [swap(after(each, *sums), "head", 1) for each in own_to_pair]
    (own,) = project_rest(
        after(head_arg, down_second, down_first),
        [[(0, at) for at in range(Y_UNITS)]],
        y_normed, output_weight, unit, 1,
    )
    up_own = ups.end(own)
    rank = up.shape[1]
    up_first, up_second = up_own[:rank], up_own[rank:]
    up_before = shift_up(up_second, "ctx", 1)
    low = low_part(
        after(turn_first_token, own, ups.got), me, y_normed, [down_before, down_first, down_second]
    )
    low = low + swap(after(low, up_before), "head", 1)
    low_sent = after(low.astype(BF16), *[arrived for arrived, _, _ in parts])
    for chip in chips:
        low = low + swap(low_sent, "head", 2 * chip).astype(F32)
    here = [each for each in parts if each[2] in first]
    held = held_sum(own, pair, here, unit)
    last = [arrived for arrived, at, _ in parts[len(here) :] if at == 0]
    return final_sum(
        turn_first_token, me, low, held, [up_before, up_first, up_second], last, Y_FIRST, unit
    )


def solution(mesh):
    in_specs = (
        P("ctx", "head"),
        P("ctx", "head"),
        P("ctx", "head"),
        P("ctx", "head"),
        P("head", "ctx"),
        P("head"),
        P("head"),
        P(None, "head"),
        P(None, "head"),
        P(None, "head"),
        P("head"),
        P("head", None),
        P("ctx", "head", None),
        P("ctx", None, "head"),
        P(),
        P(),
        P(),
    )
    out_specs = P("ctx", "head")
    return jax.shard_map(local, mesh=mesh, in_specs=in_specs, out_specs=out_specs, check_vma=False)
```

```python
import functools

import jax
import jax.numpy as jnp
import ml_dtypes
import numpy as np
from jax import lax
from jax.experimental import pallas as pl
from jax.experimental.pallas import tpu as pltpu
from jax.sharding import PartitionSpec as P

P_SIZE = 64
N = 128
K = 4
Q = 128
TURN_DEV = 2
HALO = 16
LANES = 128
PIECES = (5, 3)
STATE_BLOCKS = 2
FINAL_BLOCKS = 2
Y_UNITS = 4
Y_FIRST = 2

F32 = jnp.float32
BF16 = jnp.bfloat16
epsilon = 1e-05
MIB = 1024 * 1024


def params(mib=28):
    return pltpu.CompilerParams(vmem_limit_bytes=mib * MIB)


def cost(microseconds):
    return pl.CostEstimate(flops=int(microseconds * 1e5), bytes_accessed=1, transcendentals=0)


def silu(v):
    half = 0.5 * v
    return half + half * jnp.tanh(half)


def conv_rows(current, previous, taps):
    rows = current.shape[0]
    joined = jnp.concatenate([previous, current], axis=0)
    total = taps[K - 1 : K] * current
    for back in range(1, K):
        total = total + taps[K - 1 - back : K - back] * pltpu.roll(joined, back, 0)[8 : 8 + rows]
    return silu(total).astype(BF16)


def two_terms(v):
    high = v.astype(BF16).astype(F32)
    return high, v - high


def column_of(row):
    size = row.shape[1]
    here = lax.broadcasted_iota(jnp.int32, (size, size), 0)
    there = lax.broadcasted_iota(jnp.int32, (size, size), 1)
    return jnp.sum(jnp.where(here == there, row, 0.0), axis=1, keepdims=True)


def pad_rows(stack):
    rows = stack.shape[0]
    if rows % LANES:
        fill = jnp.zeros((LANES - rows % LANES, stack.shape[1]), F32)
        stack = jnp.concatenate([stack, fill], axis=0)
    return stack


def edge_kernel(x_ref, b_ref, c_ref, out_ref):
    place = 0
    for ref in (x_ref, b_ref, c_ref):
        out_ref[:, place : place + ref.shape[1]] = ref[...]
        place += ref.shape[1]


def sequence_edge(*arrays):
    tokens = arrays[0].shape[0]
    width = sum(array.shape[1] for array in arrays)
    return pl.pallas_call(
        edge_kernel,
        grid=(1,),
        in_specs=[
            pl.BlockSpec((HALO, array.shape[1]), lambda i: (tokens // HALO - 1, 0)) for array in arrays
        ],
        out_specs=pl.BlockSpec((HALO, width), lambda i: (0, 0)),
        out_shape=jax.ShapeDtypeStruct((HALO, width), BF16),
        compiler_params=params(62),
        cost_estimate=cost(1),
        name="sequence_edge",
    )(*arrays)


def panel_home(place, panel_index, tenants, me, *, bits, slot, count):
    relative = 0
    for order, bit in enumerate(bits):
        relative += bit * (1 - (place >> (len(bits) - 1 - order)) % 2)
    panel = panel_index[tenants[TURN_DEV * (relative ^ me) + slot]]
    owned = lax.div(panel, count) == me
    return jnp.where(owned, lax.rem(panel, count), 0), owned


def panel_kernel(homes, devices, index_ref, tenant_ref, me_ref, *refs):
    ins, outs = refs[: len(homes)], refs[len(homes) : 3 * len(homes)]
    zeros, sems = refs[-2:]
    zeros[...] = jnp.zeros_like(zeros)
    half = devices // 2
    started = []
    for number, job in enumerate(homes):
        in_ref = ins[number]
        rows, width = in_ref.shape[1:]
        for place in range(devices):
            out_ref = outs[2 * number + (place >= half)]
            for slot, home in enumerate(job):
                local, owned = home(place, index_ref, tenant_ref, me_ref[0])
                out = out_ref.at[place % half, pl.ds(slot * rows, rows), :]
                sem = sems.at[len(started)]
                own = pltpu.make_async_copy(in_ref.at[local], out, sem)
                none = pltpu.make_async_copy(zeros.at[pl.ds(0, rows), pl.ds(0, width)], out, sem)

                @pl.when(owned)
                def _(own=own):
                    own.start()

                @pl.when(jnp.logical_not(owned))
                def _(none=none):
                    none.start()

                started.append(none)
    for copy in started:
        copy.wait()


def pack_panels(jobs, panel_index, tenants, me, devices):
    half = devices // 2
    homes, out_shape, copies = [], [], 0
    for panels, bits, slots in jobs:
        count, rows, width = panels.shape
        homes.append(
            [
                functools.partial(panel_home, bits=bits, slot=slot, count=count)
                for slot in slots
            ]
        )
        out_shape += [jax.ShapeDtypeStruct((half, len(slots) * rows, width), BF16)] * 2
        copies += devices * len(slots)
    zero_shape = tuple(max(panels.shape[axis] for panels, _, _ in jobs) for axis in (1, 2))
    outs = pl.pallas_call(
        functools.partial(panel_kernel, homes, devices),
        grid_spec=pltpu.PrefetchScalarGridSpec(
            num_scalar_prefetch=3,
            grid=(1,),
            in_specs=[pl.BlockSpec(job[0].shape, lambda i, *_: (0, 0, 0)) for job in jobs],
            out_specs=[pl.BlockSpec(memory_space=pl.ANY)] * len(out_shape),
            scratch_shapes=[pltpu.VMEM(zero_shape, BF16), pltpu.SemaphoreType.DMA((copies,))],
        ),
        out_shape=out_shape,
        compiler_params=params(50),
        cost_estimate=cost(5),
        name="pack_panels",
    )(panel_index, tenants, me, *[job[0] for job in jobs])
    return [outs[2 * job : 2 * job + 2] for job in range(len(jobs))]


def state_kernel(
    parity_ref, x_ref, b_ref, even_ref, odd_ref, raw_ref, rate_ref, xt_ref, bt_ref, spread_ref,
    xc_ref, bc_ref, run_ref, shifted_ref, before_ref, start_ref, keep_ref, send_ref,
    x_prev, b_prev, weight, x_weighted, state, decay_product,
):
    block = pl.program_id(0)
    inner = x_ref.shape[1]
    bc_width = b_ref.shape[1]
    groups = bc_width // N
    width = inner // groups

    @pl.when(block == 0)
    def _():
        halo = jnp.where(parity_ref[0] == 1, even_ref[...], odd_ref[...])
        x_prev[...] = halo[:, :inner].astype(F32)[8:]
        b_prev[...] = halo[:, inner : inner + bc_width].astype(F32)[8:]
        state[...] = jnp.zeros_like(state)
        decay_product[...] = jnp.ones_like(decay_product)

    raw = raw_ref[...]
    step = jnp.maximum(raw, 0.0) + jnp.log1p(jnp.exp(-jnp.abs(raw)))
    change = -step * jnp.exp(column_of(rate_ref[...]))
    heads = raw.shape[0]
    first = change.astype(BF16)
    rest = change - first.astype(F32)
    second = rest.astype(BF16)
    third = (rest - second.astype(F32)).astype(BF16)
    terms = jnp.concatenate([first, second, third], axis=0)
    upper = (
        lax.broadcasted_iota(jnp.int32, (Q, Q), 0) <= lax.broadcasted_iota(jnp.int32, (Q, Q), 1)
    ).astype(F32).astype(BF16)
    spread = spread_ref[...]
    parts = [slice(part * Q, (part + 1) * Q) for part in range(STATE_BLOCKS)]
    decay_rows = []
    for rows in parts:
        sums = jnp.dot(terms[:, rows], upper, preferred_element_type=F32)
        run = sums[:heads] + sums[heads : 2 * heads] + sums[2 * heads :]
        run_ref[:, rows] = run
        shifted_ref[:, rows] = jnp.log(step[:, rows]) - run
        last = run[:, Q - 1 : Q]
        tail = jnp.exp(last - run) * step[:, rows]
        whole = jnp.broadcast_to(jnp.exp(last), (heads, Q))
        columns = pad_rows(jnp.concatenate([*two_terms(tail), *two_terms(whole)], axis=0)).T
        weight[rows, :] = jnp.dot(
            columns[:, : 2 * heads].astype(BF16), spread, preferred_element_type=F32
        )
        decay_rows.append(
            jnp.dot(columns[:16, 2 * heads : 4 * heads].astype(BF16), spread, preferred_element_type=F32)[:8]
        )

    bc = conv_rows(b_ref[...].astype(F32), b_prev[...], bt_ref[...].astype(F32))
    b_prev[...] = b_ref[STATE_BLOCKS * Q - HALO :, :].astype(F32)[8:]
    bc_ref[...] = bc

    def conv_lanes(part, carried):
        lanes = pl.ds(pl.multiple_of(part * LANES, LANES), LANES)
        current = x_ref[:, lanes].astype(F32)
        xc = conv_rows(current, x_prev[:, lanes], xt_ref[:, lanes].astype(F32))
        x_prev[:, lanes] = current[STATE_BLOCKS * Q - 8 :]
        xc_ref[:, lanes] = xc
        x_weighted[:, lanes] = (xc.astype(F32) * weight[:, lanes]).astype(BF16)
        return carried

    lax.fori_loop(0, inner // LANES, conv_lanes, 0, unroll=16)

    for part, (rows, decay_row) in enumerate(zip(parts, decay_rows)):
        start_ref[part * 8 : (part + 1) * 8, :] = decay_product[...]
        decay_product[...] = decay_product[...] * decay_row
        for group in range(groups):
            lanes = slice(group * width, (group + 1) * width)
            fresh = lax.dot_general(
                bc[rows, group * N : (group + 1) * N],
                x_weighted[rows, lanes],
                (((0,), (0,)), ((), ())),
                preferred_element_type=F32,
            )
            held = state[:, lanes]
            before_ref[part * N : (part + 1) * N, lanes] = held.astype(BF16)
            state[:, lanes] = held * decay_row[:1, lanes] + fresh

    @pl.when(block == pl.num_programs(0) - 1)
    def _():
        half = inner // 2
        row = lax.broadcasted_iota(jnp.int32, (HALO, half), 0)
        for out_ref, place in ((keep_ref, parity_ref[0]), (send_ref, 1 - parity_ref[0])):
            lanes = pl.ds(pl.multiple_of(place * half, LANES), half)
            out_ref[:N] = state[:, lanes].astype(BF16)
            high, low = two_terms(decay_product[:1, lanes])
            out_ref[N:] = jnp.where(row == 0, high, jnp.where(row == 1, low, 0.0)).astype(BF16)


def local_states(parity, x, b, halos, raw, rate, x_taps, b_taps, spread):
    tokens, inner = x.shape
    bc_width = b.shape[1]
    heads = raw.shape[0]
    blocks = tokens // Q
    half = inner // 2
    span = STATE_BLOCKS * Q
    whole = lambda c, p: (0, 0)
    rows = lambda c, p: (c, 0)
    columns = lambda c, p: (0, c)
    return pl.pallas_call(
        state_kernel,
        grid_spec=pltpu.PrefetchScalarGridSpec(
            num_scalar_prefetch=1,
            grid=(blocks // STATE_BLOCKS,),
            in_specs=[
                pl.BlockSpec((span, inner), rows),
                pl.BlockSpec((span, bc_width), rows),
                pl.BlockSpec(halos[0].shape, whole),
                pl.BlockSpec(halos[0].shape, whole),
                pl.BlockSpec((heads, span), columns),
                pl.BlockSpec((1, heads), whole),
                pl.BlockSpec((K, inner), whole),
                pl.BlockSpec((K, bc_width), whole),
                pl.BlockSpec(spread.shape, whole),
            ],
            out_specs=[
                pl.BlockSpec((span, inner), rows),
                pl.BlockSpec((span, bc_width), rows),
                pl.BlockSpec((heads, span), columns),
                pl.BlockSpec((heads, span), columns),
                pl.BlockSpec((STATE_BLOCKS * N, inner), rows),
                pl.BlockSpec((STATE_BLOCKS * 8, inner), rows),
                pl.BlockSpec((N + HALO, half), whole),
                pl.BlockSpec((N + HALO, half), whole),
            ],
            scratch_shapes=[
                pltpu.VMEM((8, inner), F32),
                pltpu.VMEM((8, bc_width), F32),
                pltpu.VMEM((span, inner), F32),
                pltpu.VMEM((span, inner), BF16),
                pltpu.VMEM((N, inner), F32),
                pltpu.VMEM((8, inner), F32),
            ],
        ),
        out_shape=[
            jax.ShapeDtypeStruct((tokens, inner), BF16),
            jax.ShapeDtypeStruct((tokens, bc_width), BF16),
            jax.ShapeDtypeStruct((heads, tokens), F32),
            jax.ShapeDtypeStruct((heads, tokens), F32),
            jax.ShapeDtypeStruct((blocks * N, inner), BF16),
            jax.ShapeDtypeStruct((blocks * 8, inner), F32),
            jax.ShapeDtypeStruct((N + HALO, half), BF16),
            jax.ShapeDtypeStruct((N + HALO, half), BF16),
        ],
        compiler_params=params(50),
        cost_estimate=cost(150000),
        name="local_states",
    )(parity, x, b, *halos, raw, rate, x_taps, b_taps, spread)


def mix_kernel(
    first, has_alias, parity_ref, *refs
):
    (
        xc_ref, bc_ref, c_ref, c_prev_ref, even_ref, odd_ref, run_ref, shifted_ref, before_ref, start_ref,
        gate_ref, skip_ref, ct_ref, spread_ref,
    ) = refs[:14]
    refs = refs[14 + (3 if has_alias else 0) :]
    part_ref, scale_ref, cc_ref, rise = refs
    block = pl.program_id(0) + first
    inner = xc_ref.shape[1]
    bc_width = c_ref.shape[1]
    groups = bc_width // N
    width = inner // groups
    heads = run_ref.shape[0]

    at = slice(inner + bc_width, inner + 2 * bc_width)
    c_halo = jnp.where(parity_ref[0] == 1, even_ref[:, at], odd_ref[:, at]).astype(F32)[8:]
    c_before = jnp.where(block == 0, c_halo, c_prev_ref[...].astype(F32)[8:])
    cc = conv_rows(c_ref[...].astype(F32), c_before, ct_ref[...].astype(F32))
    cc_ref[...] = cc
    run = run_ref[...]
    columns = pad_rows(jnp.concatenate([*two_terms(jnp.exp(run)), run], axis=0)).T
    rise[...] = jnp.dot(
        columns[:, : 2 * heads].astype(BF16), spread_ref[...], preferred_element_type=F32
    )
    skips = jnp.broadcast_to(jnp.concatenate(two_terms(skip_ref[...]), axis=1), (16, 2 * heads))
    skip = jnp.dot(skips.astype(BF16), spread_ref[...], preferred_element_type=F32)[:1]
    causal = lax.broadcasted_iota(jnp.int32, (Q, Q), 0) >= lax.broadcasted_iota(jnp.int32, (Q, Q), 1)
    left = lax.broadcasted_iota(jnp.int32, (Q, LANES), 1) < P_SIZE
    for group in range(groups):
        state_lanes = slice(group * N, (group + 1) * N)
        scores = lax.dot_general(
            cc[:, state_lanes],
            bc_ref[:, state_lanes],
            (((1,), (1,)), ((), ())),
            preferred_element_type=F32,
        )
        scores = jnp.where(causal, scores, 0.0)
        for pair in range(width // LANES):
            lanes = slice(group * width + pair * LANES, group * width + (pair + 1) * LANES)
            mixing = []
            for head in (lanes.start // P_SIZE, lanes.start // P_SIZE + 1):
                gap = columns[:, 2 * heads + head : 2 * heads + head + 1] + shifted_ref[head : head + 1, :]
                mixing.append((scores * jnp.exp(jnp.where(causal, gap, 0.0))).astype(BF16))
            x = xc_ref[:, lanes].astype(F32)
            x_pair = jnp.concatenate(
                [jnp.where(left, x, 0.0).astype(BF16), jnp.where(left, 0.0, x).astype(BF16)], axis=0
            )
            y = jnp.dot(jnp.concatenate(mixing, axis=1), x_pair, preferred_element_type=F32)
            carried = jnp.dot(cc[:, state_lanes], before_ref[:, lanes], preferred_element_type=F32)
            rise_part = rise[:, lanes]
            y = y + rise_part * carried + skip[:, lanes] * x
            gate = silu(gate_ref[:, lanes].astype(F32))
            part_ref[:, lanes] = (y * gate).astype(BF16)
            scale_ref[:, lanes] = (gate * rise_part * start_ref[:1, lanes]).astype(BF16)


def mix(
    first, count, parity, xc, bc, c, halos, run, shifted, before, start, gate, skip, c_taps, spread, held
):
    tokens, inner = xc.shape
    bc_width = c.shape[1]
    heads = run.shape[0]
    whole = lambda i, p: (0, 0)
    rows = lambda i, p: (first + i, 0)
    columns = lambda i, p: (0, first + i)
    per_block = Q // HALO
    any_spec = pl.BlockSpec(memory_space=pl.ANY)
    aliased = list(held) if held is not None else []
    return pl.pallas_call(
        functools.partial(mix_kernel, first, bool(aliased)),
        grid_spec=pltpu.PrefetchScalarGridSpec(
            num_scalar_prefetch=1,
            grid=(count,),
            in_specs=[
                pl.BlockSpec((Q, inner), rows),
                pl.BlockSpec((Q, bc_width), rows),
                pl.BlockSpec((Q, bc_width), rows),
                pl.BlockSpec(
                    (HALO, bc_width), lambda i, p: (jnp.maximum((first + i) * per_block - 1, 0), 0)
                ),
                pl.BlockSpec(halos[0].shape, whole),
                pl.BlockSpec(halos[0].shape, whole),
                pl.BlockSpec((heads, Q), columns),
                pl.BlockSpec((heads, Q), columns),
                pl.BlockSpec((N, inner), rows),
                pl.BlockSpec((8, inner), rows),
                pl.BlockSpec((Q, inner), rows),
                pl.BlockSpec((1, heads), whole),
                pl.BlockSpec((K, bc_width), whole),
                pl.BlockSpec(spread.shape, whole),
            ]
            + [any_spec] * len(aliased),
            out_specs=[
                pl.BlockSpec((Q, inner), rows),
                pl.BlockSpec((Q, inner), rows),
                pl.BlockSpec((Q, bc_width), rows),
            ],
            scratch_shapes=[pltpu.VMEM((Q, inner), F32)],
        ),
        out_shape=[
            jax.ShapeDtypeStruct((tokens, inner), BF16),
            jax.ShapeDtypeStruct((tokens, inner), BF16),
            jax.ShapeDtypeStruct((tokens, bc_width), BF16),
        ],
        input_output_aliases={15 + i: i for i in range(len(aliased))},
        compiler_params=params(50),
        cost_estimate=cost(count * 25000),
        name="mix",
    )(parity, xc, bc, c, c, *halos, run, shifted, before, start, gate, skip, c_taps, spread, *aliased)


def project_unit(y_ref, w_ref, send_ref, keep_ref, step, units):
    @pl.when(step < units)
    def _():
        send_ref[...] = jnp.dot(y_ref[...], w_ref[...], preferred_element_type=F32).astype(BF16)

    @pl.when(step >= units)
    def _():
        keep_ref[...] = jnp.dot(y_ref[...], w_ref[...], preferred_element_type=F32).astype(BF16)


def norm_kernel(
    tiles, parity_ref, place_ref, part_ref, scale_ref, cc_ref, keep_state_ref, got_ref, gain_ref, w_ref,
    out_ref, send_ref, keep_ref, state,
):
    inner = part_ref.shape[1]
    groups = cc_ref.shape[1] // N
    width = inner // groups
    half = inner // 2
    step = pl.program_id(0)
    tile = part_ref.shape[0]

    @pl.when(step == 0)
    def _():
        for ref, place in ((keep_state_ref, parity_ref[0]), (got_ref, 1 - parity_ref[0])):
            state[:, pl.ds(pl.multiple_of(place * half, LANES), half)] = ref[...]

    @pl.when(step < tiles)
    def _():
        rows = pl.ds(pl.multiple_of(step * tile, tile), tile)
        for group in range(groups):
            lanes = slice(group * width, (group + 1) * width)
            carried = jnp.dot(
                cc_ref[:, group * N : (group + 1) * N], state[:, lanes], preferred_element_type=F32
            )
            gated = part_ref[:, lanes].astype(F32) + scale_ref[:, lanes].astype(F32) * carried
            mean = jnp.sum(gated * gated, axis=1, keepdims=True) * (1.0 / width)
            normed = gated * lax.rsqrt(mean + epsilon) * gain_ref[:, lanes].astype(F32)
            out_ref[rows, lanes] = normed.astype(BF16)

    @pl.when(step >= tiles)
    def _():
        project_unit(out_ref, w_ref, send_ref, keep_ref, step - tiles, pl.num_programs(0) // 2 - tiles // 2)


def norm_project(parity, head, blocks, part, scale, cc, keep, got, gain, weight, width):
    tokens, inner = part.shape
    tile = 2 * Q
    tiles = tokens // tile
    units = len(blocks) // 2
    place = place_of(blocks)
    whole = lambda i, p, q: (0, 0)
    rows = lambda i, p, q: (jnp.minimum(i, tiles - 1), 0)
    return pl.pallas_call(
        functools.partial(norm_kernel, tiles),
        grid_spec=pltpu.PrefetchScalarGridSpec(
            num_scalar_prefetch=2,
            grid=(tiles + 2 * units,),
            in_specs=[
                pl.BlockSpec((tile, inner), rows),
                pl.BlockSpec((tile, inner), rows),
                pl.BlockSpec((tile, cc.shape[1]), rows),
                pl.BlockSpec(keep.shape, whole),
                pl.BlockSpec(got.shape, whole),
                pl.BlockSpec((1, inner), whole),
                pl.BlockSpec((inner, width), lambda i, p, q: (0, place(jnp.maximum(i - tiles, 0), q[0]))),
            ],
            out_specs=[
                pl.BlockSpec((tokens, inner), whole),
                pl.BlockSpec((tokens, width), lambda i, p, q: (0, jnp.clip(i - tiles, 0, units - 1))),
                pl.BlockSpec((tokens, width), lambda i, p, q: (0, jnp.maximum(i - tiles - units, 0))),
            ],
            scratch_shapes=[pltpu.VMEM((N, inner), BF16)],
        ),
        out_shape=[
            jax.ShapeDtypeStruct((tokens, inner), BF16),
            jax.ShapeDtypeStruct((tokens, units * width), BF16),
            jax.ShapeDtypeStruct((tokens, units * width), BF16),
        ],
        compiler_params=params(50),
        cost_estimate=cost(11),
        name="norm_project",
    )(parity, head, part, scale, cc, keep, got, gain, weight)


def place_of(blocks):
    def column(step, head):
        column = (head ^ blocks[0][0]) * Y_UNITS + blocks[0][1]
        for index, (bits, unit) in enumerate(blocks[1:], 1):
            column = jnp.where(step == index, (head ^ bits) * Y_UNITS + unit, column)
        return column

    return column


def rest_kernel(counts, head_ref, y_ref, w_ref, *outs):
    step = pl.program_id(0)
    start = 0
    for count, out_ref in zip(counts, outs):

        @pl.when((step >= start) & (step < start + count))
        def _(out_ref=out_ref):
            out_ref[...] = jnp.dot(y_ref[...], w_ref[...], preferred_element_type=F32).astype(BF16)

        start += count


def project_rest(head, sides, y, weight, width, microseconds):
    tokens, inner = y.shape
    counts = [len(side) for side in sides]
    blocks = [block for side in sides for block in side]
    place = place_of(blocks)
    out_specs, start = [], 0
    for count in counts:
        out_specs.append(
            pl.BlockSpec(
                (tokens, width),
                lambda i, p, start=start, count=count: (0, jnp.clip(i - start, 0, count - 1)),
            )
        )
        start += count
    return pl.pallas_call(
        functools.partial(rest_kernel, counts),
        grid_spec=pltpu.PrefetchScalarGridSpec(
            num_scalar_prefetch=1,
            grid=(len(blocks),),
            in_specs=[
                pl.BlockSpec((tokens, inner), lambda i, p: (0, 0)),
                pl.BlockSpec((inner, width), lambda i, p: (0, place(i, p[0]))),
            ],
            out_specs=out_specs,
        ),
        out_shape=[jax.ShapeDtypeStruct((tokens, count * width), BF16) for count in counts],
        compiler_params=params(46),
        cost_estimate=cost(microseconds),
        name="project_rest",
    )(head, y, weight)


def block_slot(block, starts, me, tokens):
    place = me * tokens + block * Q
    slot = 0
    for turn in range(TURN_DEV):
        slot = slot + (starts[TURN_DEV * me + turn] <= place).astype(jnp.int32)
    return slot


def chosen(slot, refs):
    panel = refs[0][...]
    for index in range(1, len(refs)):
        panel = jnp.where(slot == index, refs[index][...], panel)
    return panel


def low_kernel(tokens, start_ref, me_ref, y_ref, *refs):
    panels, out_ref = refs[:-1], refs[-1]
    fold = Q // 2
    for block in range(FINAL_BLOCKS):
        slot = block_slot(pl.program_id(0) * FINAL_BLOCKS + block, start_ref, me_ref[0], tokens)
        low = lax.dot_general(
            y_ref[block * Q : (block + 1) * Q, :],
            chosen(slot, panels),
            (((1,), (1,)), ((), ())),
            preferred_element_type=F32,
        )
        out_ref[block * fold : (block + 1) * fold, :] = jnp.concatenate([low[:fold], low[fold:]], axis=1)


def low_part(starts, me, y, panels):
    tokens, inner = y.shape
    span = FINAL_BLOCKS * Q
    rows = lambda i, s, m: (i, 0)
    whole = lambda i, s, m: (0, 0)
    return pl.pallas_call(
        functools.partial(low_kernel, tokens),
        grid_spec=pltpu.PrefetchScalarGridSpec(
            num_scalar_prefetch=2,
            grid=(tokens // span,),
            in_specs=[pl.BlockSpec((span, inner), rows)]
            + [pl.BlockSpec(panel.shape, whole) for panel in panels],
            out_specs=pl.BlockSpec((span // 2, LANES), rows),
        ),
        out_shape=jax.ShapeDtypeStruct((tokens // 2, LANES), F32),
        compiler_params=params(46),
        cost_estimate=cost(4),
        name="low_part",
    )(starts, me, y, *panels)


def held_kernel(counts, unit, *refs):
    own, pair = refs[:Y_UNITS], refs[Y_UNITS : 2 * Y_UNITS]
    parts, out_ref = list(refs[2 * Y_UNITS : -1]), refs[-1]
    for block in range(Y_UNITS):
        total = own[block][...].astype(F32) + pair[block][...].astype(F32)
        for _ in range(counts[block]):
            total = total + parts.pop(0)[...].astype(F32)
        out_ref[:, block * unit : (block + 1) * unit] = total


def held_sum(own, pair, parts, unit):
    tokens = own.shape[0]
    tile = 2 * Q
    column = lambda at: pl.BlockSpec((tile, unit), lambda i: (i, at))
    here = [[(array, at) for array, at, block in parts if block == unit_at] for unit_at in range(Y_UNITS)]
    return pl.pallas_call(
        functools.partial(held_kernel, [len(each) for each in here], unit),
        grid=(tokens // tile,),
        in_specs=[column(block) for block in range(Y_UNITS)]
        + [column(0)] * Y_UNITS
        + [column(at) for each in here for _, at in each],
        out_specs=pl.BlockSpec((tile, Y_UNITS * unit), lambda i: (i, 0)),
        out_shape=jax.ShapeDtypeStruct((tokens, Y_UNITS * unit), F32),
        compiler_params=params(),
        cost_estimate=cost(3),
        name="held_sum",
    )(*[own] * Y_UNITS, *pair, *[array for each in here for array, _ in each])


def final_kernel(tokens, first, unit, start_ref, me_ref, low_ref, held_ref, *refs):
    panels, parts, out_ref = refs[: TURN_DEV + 1], refs[TURN_DEV + 1 : -1], refs[-1]
    rank = LANES // 2
    start = first * unit
    for block in range(FINAL_BLOCKS):
        slot = block_slot(pl.program_id(0) * FINAL_BLOCKS + block, start_ref, me_ref[0], tokens)
        low = low_ref[block * Q // 2 : (block + 1) * Q // 2, :].astype(BF16)
        low = jnp.concatenate([low[:, :rank], low[:, rank:]], axis=0)
        rows = slice(block * Q, (block + 1) * Q)
        total = held_ref[rows, :] + jnp.dot(low, chosen(slot, panels), preferred_element_type=F32)
        out_ref[rows, :start] = total[:, :start].astype(BF16)
        rest = total[:, start:]
        for part in parts:
            rest = rest + part[rows, :].astype(F32)
        out_ref[rows, start:] = rest.astype(BF16)


def final_sum(starts, me, low, held, panels, parts, first, unit):
    tokens, features = held.shape
    span = FINAL_BLOCKS * Q
    rows = lambda i, s, m: (i, 0)
    whole = lambda i, s, m: (0, 0)
    return pl.pallas_call(
        functools.partial(final_kernel, tokens, first, unit),
        grid_spec=pltpu.PrefetchScalarGridSpec(
            num_scalar_prefetch=2,
            grid=(tokens // span,),
            in_specs=[pl.BlockSpec((span // 2, LANES), rows), pl.BlockSpec((span, features), rows)]
            + [pl.BlockSpec(panel.shape, whole) for panel in panels]
            + [pl.BlockSpec((span, part.shape[1]), rows) for part in parts],
            out_specs=pl.BlockSpec((span, features), rows),
        ),
        out_shape=jax.ShapeDtypeStruct((tokens, features), BF16),
        compiler_params=params(),
        cost_estimate=cost(3),
        name="final_sum",
    )(starts, me, low, held, *panels, *parts)


def shift_up(block, axis, distance):
    devices = range(lax.axis_size(axis))
    route = [(i, i + distance) for i in devices if i + distance in devices]
    return lax.ppermute(block, axis, route)


def swap(block, axis, bits):
    return lax.ppermute(block, axis, [(i, i ^ bits) for i in range(lax.axis_size(axis))])


def after(value, *earlier):
    return lax.optimization_barrier((value, *earlier))[0] if earlier else value


def neighbour_edge(edge):
    size = lax.axis_size("ctx")
    even = lax.ppermute(edge, "ctx", [(i, i ^ 1) for i in range(size)])
    odd = lax.ppermute(edge, "ctx", [(i, i + 1 if i % 2 else i - 1) for i in range(1, size - 1)])
    return even, odd


class Route:
    def __init__(self, bits, send, keep):
        self.bits, self.send, self.held, self.size = list(bits), send, [keep], keep.shape[0]
        self.got = None

    def merge(self, *earlier):
        self.held.append(after(self.got, *earlier))
        half = self.size // 2
        self.send = sum(each[each.shape[0] - self.size : each.shape[0] - half] for each in self.held)
        self.size, self.got = half, None
        return self.send

    def step(self, *earlier):
        if not self.bits:
            return
        if self.got is not None:
            self.merge(*earlier)
        self.got = swap(after(self.send, *earlier), "ctx", self.bits.pop(0))

    def end(self, *earlier):
        while self.bits:
            self.step(*earlier)
        self.held.append(after(self.got, *earlier))
        return sum(each[-1] for each in self.held)


def unpacked(packed):
    decay = packed[N : N + 1].astype(F32) + packed[N + 1 : N + 2].astype(F32)
    return packed[:N].astype(F32), decay


def packed(state, decay):
    high = decay.astype(BF16)
    low = (decay - high.astype(F32)).astype(BF16)
    fill = jnp.zeros((HALO - 2, state.shape[1]), BF16)
    return jnp.concatenate([state.astype(BF16), high, low, fill], axis=0)


def local(
    input_x_channels,
    input_b_channels,
    input_c_channels,
    input_gate_channels,
    raw_step_sizes,
    log_decay_rate,
    head_skip_coeff,
    x_conv_taps,
    b_conv_taps,
    c_conv_taps,
    gated_norm_gain,
    output_weight,
    adapter_down_panels,
    adapter_up_panels,
    turn_first_token,
    tenant_of_turn,
    tenant_panel_index,
):
    tokens, inner = input_x_channels.shape
    heads = log_decay_rate.shape[0]
    blocks = tokens // Q
    features = adapter_up_panels.shape[2]
    unit = features // Y_UNITS
    ctx = lax.axis_index("ctx").astype(jnp.int32)
    head = lax.axis_index("head").astype(jnp.int32)
    devices = lax.axis_size("ctx")
    parity = ctx % 2
    first = parity == 0
    me = ctx[None]
    parity_arg, head_arg = parity[None], head[None]
    down = jnp.swapaxes(adapter_down_panels, 1, 2)
    up = adapter_up_panels
    outer = [1 << bit for bit in range(1, devices.bit_length() - 1)]
    near, far = [1] + outer, outer + [1]

    edge = sequence_edge(input_x_channels, input_b_channels, input_c_channels)
    halos = neighbour_edge(edge)

    slots = range(TURN_DEV)

    def pack(jobs, *earlier):
        packs = pack_panels(jobs, tenant_panel_index, tenant_of_turn, after(me, *earlier), devices)
        return [Route(bits, *each) for (_, bits, _), each in zip(jobs, packs)]

    down_early, down_late, ups = pack(
        [(down, far, slots[:1]), (down, near, slots[1:]), (up, near, slots)]
    )
    packed_first = down_early.send
    down_early.step()
    down_late.step()

    lane_head = np.arange(inner) // P_SIZE
    spread = jnp.asarray(
        (np.arange(2 * heads)[:, None] % heads == lane_head[None, :]).astype(ml_dtypes.bfloat16)
    )
    xc, bc, run, shifted, before, start, keep, send = local_states(
        after(parity_arg, packed_first),
        input_x_channels,
        input_b_channels,
        halos,
        raw_step_sizes,
        log_decay_rate[None],
        x_conv_taps,
        b_conv_taps,
        spread,
    )
    cuts = [blocks * sum(PIECES[:piece]) // sum(PIECES) for piece in range(len(PIECES) + 1)]

    def mix_piece(piece, held, *earlier):
        return mix(
            cuts[piece], cuts[piece + 1] - cuts[piece], after(parity_arg, *earlier), xc, bc, input_c_channels, halos, run, shifted,
            before, start, input_gate_channels, head_skip_coeff[None], c_conv_taps, spread, held,
        )

    got = swap(send, "ctx", 1)
    held = mix_piece(0, None, send)
    got = after(got, held[2])
    own_state, own_decay = unpacked(keep)
    got_state, got_decay = unpacked(got)
    first_state = jnp.where(first, own_state, got_state)
    first_decay = jnp.where(first, own_decay, got_decay)
    total = jnp.where(first, got_state, own_state)
    total_decay = jnp.where(first, got_decay, own_decay)
    total, total_decay = total + total_decay * first_state, total_decay * first_decay
    ups.step(got)
    incoming = jnp.zeros_like(total)
    incoming_decay = jnp.ones_like(total_decay)
    for bit in outer:
        sent = packed(total, total_decay)
        got = swap(sent, "ctx", bit)
        if bit == outer[0]:
            got = after(got, down_early.merge(sent), down_late.merge(sent))
        if bit == outer[-1]:
            held = mix_piece(1, held, sent)
            got = after(got, held[2])
        state, decay = unpacked(got)
        upper = (ctx & bit) != 0
        incoming = jnp.where(upper, incoming + incoming_decay * state, incoming)
        incoming_decay = jnp.where(upper, incoming_decay * decay, incoming_decay)
        total, total_decay = (
            jnp.where(upper, total + total_decay * state, state + decay * total),
            total_decay * decay,
        )
    down_early.step(held[2])
    down_late.step(held[2])
    incoming_second = first_state + first_decay * incoming
    back_sent = jnp.where(first, incoming_second, incoming).astype(BF16)
    kept = jnp.where(first, incoming, incoming_second).astype(BF16)
    back = swap(back_sent, "ctx", 1)
    part, scale, cc = held

    chips = range(1, lax.axis_size("head") // 2)
    first, later = range(Y_FIRST), range(Y_FIRST, Y_UNITS)

    def side(units, core):
        return [(2 * chip ^ core, at) for chip in chips for at in units]

    parts = []

    def send_both(mine, to_pair, units, *earlier):
        from_pair = swap(after(to_pair, *earlier), "head", 1)
        sums = []
        for chip in chips:
            columns = slice((chip - 1) * len(units) * unit, chip * len(units) * unit)
            both = (mine[:, columns].astype(F32) + from_pair[:, columns].astype(F32)).astype(BF16)
            arrived = swap(both, "head", 2 * chip)
            parts.extend((arrived, at - units.start, at) for at in units)
            sums.append(both)
        return sums

    routes = (down_late, down_early, ups)
    y_normed, to_pair, mine = norm_project(
        parity_arg, head_arg, side(first, 1) + side(first, 0), part, scale, cc, kept, back,
        gated_norm_gain[None], output_weight, unit,
    )
    sums = send_both(mine, to_pair, first, down_early.got, down_late.got, ups.got)
    down_late.step(*sums)
    down_early.step(*sums)
    ups.step(*sums)
    to_pair, mine, *own_to_pair = project_rest(
        after(head_arg, *sums),
        [side(later, 1), side(later, 0)] + [[(1, at)] for at in range(Y_UNITS)],
        y_normed, output_weight, unit, 1,
    )
    sums = send_both(
        mine, to_pair, later,
        *[arrived for arrived, _, _ in parts], down_early.got, down_late.got, ups.got,
    )
    ups.step(*sums)
    down_second = down_late.end(*sums)
    down_first = down_early.end(*sums)
    down_before = shift_up(down_second, "ctx", 1)
    pair = [swap(after(each, *sums), "head", 1) for each in own_to_pair]
    (own,) = project_rest(
        after(head_arg, down_second, down_first),
        [[(0, at) for at in range(Y_UNITS)]],
        y_normed, output_weight, unit, 1,
    )
    up_own = ups.end(own)
    rank = up.shape[1]
    up_first, up_second = up_own[:rank], up_own[rank:]
    up_before = shift_up(up_second, "ctx", 1)
    low = low_part(
        after(turn_first_token, own, ups.got), me, y_normed, [down_before, down_first, down_second]
    )
    low = low + swap(after(low, up_before), "head", 1)
    low_sent = after(low.astype(BF16), *[arrived for arrived, _, _ in parts])
    for chip in chips:
        low = low + swap(low_sent, "head", 2 * chip).astype(F32)
    here = [each for each in parts if each[2] in first]
    held = held_sum(own, pair, here, unit)
    last = [arrived for arrived, at, _ in parts[len(here) :] if at == 0]
    return final_sum(
        turn_first_token, me, low, held, [up_before, up_first, up_second], last, Y_FIRST, unit
    )


def solution(mesh):
    in_specs = (
        P("ctx", "head"),
        P("ctx", "head"),
        P("ctx", "head"),
        P("ctx", "head"),
        P("head", "ctx"),
        P("head"),
        P("head"),
        P(None, "head"),
        P(None, "head"),
        P(None, "head"),
        P("head"),
        P("head", None),
        P("ctx", "head", None),
        P("ctx", None, "head"),
        P(),
        P(),
        P(),
    )
    out_specs = P("ctx", "head")
    return jax.shard_map(local, mesh=mesh, in_specs=in_specs, out_specs=out_specs, check_vma=False)
```
